32 devices in a mesh: dp: 2 (over x), tensor: 8 (over z, y), group: 2 (over core).
Axes of the slice: x: 2, y: 2, z: 4, core: 2. Of those that a mesh axis runs over, the one named last changes fastest.
Arguments:
- resid: bfloat16 [256, 4096], P('dp'), may hold values from -6 to 6
- mixer_out: bfloat16 [256, 8192], P('dp', ('tensor', 'group')), may hold values from -6 to 6
- out_proj: bfloat16 [8192, 4096], P(('tensor', 'group')), may hold values from -0.0625 to 0.0625
- norm_gain: float32 [4096], replicated, may hold values from 0.1 to 1.9
- router: float32 [4096, 4], replicated, may hold values from -0.09375 to 0.09375
- routes: int32 [256, 2], P('dp'), may hold values from 0 to 3, all different within a row; in each aligned block of 128 rows (0 to 127, 128 to 255, ...) at most 96 rows name the same one
- w_gate: bfloat16 [8, 4096, 3584], P('tensor', None, ('dp', 'group')), may hold values from -0.09375 to 0.09375
- w_up: bfloat16 [8, 4096, 3584], P('tensor', None, ('dp', 'group')), may hold values from -0.09375 to 0.09375
- w_down: bfloat16 [8, 3584, 4096], P('tensor', ('dp', 'group')), may hold values from -0.0625 to 0.0625
- cotangent: bfloat16 [256, 4096], P('dp'), may hold values from -6 to 6
Outputs:
- layer_out: bfloat16 [256, 4096], P('dp')
- grad_mixer: bfloat16 [256, 8192], P('dp', ('tensor', 'group'))
- grad_down: bfloat16 [8, 3584, 4096], P('tensor', ('dp', 'group'))
The draws below stay inside these ranges and needn't reach their ends.
Inputs may be any that keep to these rules, and one draw needn't show every extreme that they name: `routes`: in each aligned block of 128 rows (the tokens of one replica) no expert is named by more than 96 rows, and some expert reaches 96 in some block; the two experts of a row differ.
All inputs are finite; a program needn't handle non-finite values.
Results may differ from the reference program's by a relative error of at most 0.03.
Values may be sent and summed in bfloat16 or wider, within the bound.
A program may use at most 128 MiB of HBM per device.

```python
import math
import jax
import jax.numpy as jnp
import numpy as np
from jax import lax

D = 4096
INNER = 8192
FF = 7168
TOK_DEV = 128
TOKENS = 256
EXPERTS = 4
CH = 512
CAP = 96
N_DP = 2
N_TENSOR = 8
N_GROUP = 2


def level_of(rng, extent, shards, low, top_value):
    gain = 1.0
    for dim, blocks in shards:
        steps = jax.random.uniform(jax.random.fold_in(jax.random.fold_in(rng, 6), dim), (blocks,), jnp.float32, low / len(shards), top_value / len(shards))
        gain = gain * jnp.repeat(jnp.exp(steps), extent[dim] // blocks).reshape((-1,) + (1,) * (len(extent) - 1 - dim))
    return gain


def assign_block(own_key, own, number, rows, number_of, top, reach, lean):
    sequence = jax.random.permutation(own_key, number_of)
    heavy_load, ordinary = load_shares(number_of, rows * top, reach, lean, True), load_shares(number_of, rows * top, reach, lean, False)
    places = jnp.arange(number_of)

    def named(tallies, turn):
        used = int((tallies > 0).sum())
        fixed = max(1, used // 4)
        shifted = fixed + (places - fixed + turn * (used - fixed)) % max(1, number_of - fixed)
        return jnp.zeros((number_of,), jnp.int32).at[sequence[jnp.where(places < fixed, places, shifted)]].set(jnp.asarray(tallies, jnp.int32))

    tallies = jnp.where(number % 4 == 0, named(heavy_load, number // 4), named(ordinary, number - number // 4 - 1))
    mixed = jax.random.permutation(jax.random.fold_in(own, 3), number_of)
    donor, receiver = mixed[0:number_of // 2 * 2:2], mixed[1:number_of // 2 * 2:2]
    margin = jnp.minimum(tallies[donor] - 1, reach - tallies[receiver]) // 2
    margin = jnp.where((donor == sequence[0]) | (receiver == sequence[0]) | (tallies[receiver] == 0), 0, jnp.maximum(margin, 0))
    shifted = jax.random.randint(jax.random.fold_in(own, 4), (number_of // 2,), 0, 1 << 20) % (margin + 1)
    tallies = tallies.at[donor].add(-shifted).at[receiver].add(shifted)
    members = jnp.searchsorted(jnp.cumsum(tallies), jnp.arange(rows * top), side="right").astype(jnp.int32)
    table = members.reshape(top, rows).T
    table = table[jax.random.permutation(jax.random.fold_in(own, 1), rows)]
    turn = jax.random.randint(jax.random.fold_in(own, 2), (rows, 1), 0, top)
    return jnp.take_along_axis(table, (jnp.arange(top)[None, :] + turn) % top, axis=1)


def load_shares(amount, total, limit, skew, full):
    weights = [(1 << 20) // math.isqrt(rank ** skew) + 1 for rank in range(1, amount + 1)]
    largest = limit if full else min(limit, max(-(-total // amount), total * weights[0] // sum(weights)))
    least = 1 if total - largest >= amount - 1 else 0
    given, spare = [largest] + [least] * (amount - 1), total - largest - least * (amount - 1)
    while spare > 0:
        free = [i for i in range(1, amount) if given[i] < largest] or [i for i in range(1, amount) if given[i] < limit]
        whole, left = sum([weights[i] for i in free]), spare
        for i in free:
            addition = min(limit - given[i], max(1, left * weights[i] // whole), spare)
            given[i] = given[i] + addition
            spare = spare - addition
    return np.array(given)


def scatter_about(key, dims, scale, limit, split=(), kind=jnp.bfloat16):
    array = scale * jax.random.normal(key, dims, jnp.float32)
    if split:
        array = array * level_of(key, dims, split, -0.22, 0.18)
    return jnp.clip(array, -limit, limit).astype(kind)


def setup_inputs(seed: int = 0) -> dict:
    seeds = jax.random.split(jax.random.key(seed), 11)
    resid = scatter_about(seeds[0], (TOKENS, D), 1.0, 6.0, ((0, 2),))
    mixer_out = scatter_about(seeds[1], (TOKENS, INNER), 1.0, 6.0, ((0, 2), (1, 16)))
    out_proj = scatter_about(seeds[2], (INNER, D), INNER ** -0.5, 0.0625, ((0, 16),))
    norm_gain = jnp.clip(1.0 + 0.18 * jax.random.normal(seeds[3], (D,), jnp.float32), 0.1, 1.9)
    router = scatter_about(seeds[4], (D, EXPERTS), D ** -0.5, 0.09375, (), jnp.float32)
    routes_keys = jax.random.split(jax.random.fold_in(seeds[5], 1), TOKENS // TOK_DEV)
    routes_turns = jax.random.permutation(jax.random.fold_in(seeds[5], 3), TOKENS // TOK_DEV)
    routes = jax.vmap(lambda own, number: assign_block(jax.random.fold_in(seeds[5], 2), own, number, TOK_DEV, EXPERTS, 2, CAP, 2))(routes_keys, routes_turns).reshape((TOKENS, 2))
    w_gate = scatter_about(seeds[6], (2 * EXPERTS, D, FF // 2), D ** -0.5, 0.09375, ((0, 8), (2, 4)))
    w_up = scatter_about(seeds[7], (2 * EXPERTS, D, FF // 2), D ** -0.5, 0.09375, ((0, 8), (2, 4)))
    w_down = scatter_about(seeds[8], (2 * EXPERTS, FF // 2, D), FF ** -0.5, 0.0625, ((0, 8), (1, 4)))
    cotangent = scatter_about(seeds[9], (TOKENS, D), 1.0, 6.0, ((0, 2),))
    return dict(resid=resid, mixer_out=mixer_out, out_proj=out_proj, norm_gain=norm_gain, router=router, routes=routes, w_gate=w_gate, w_up=w_up, w_down=w_down, cotangent=cotangent)


def contract_rows(left, right):
    return lax.dot_general(left, right, (((0,), (0,)), ((), ())), preferred_element_type=jnp.float32)

def contract_cols(left, right):
    return lax.dot_general(left, right, (((1,), (1,)), ((), ())), preferred_element_type=jnp.float32)

def norm_forward(hidden, norm_gain):
    inv_rms = lax.rsqrt(lax.optimization_barrier(jnp.mean(hidden * hidden, axis=1, keepdims=True)) + 1e-05)
    return ((hidden * inv_rms * norm_gain).astype(jnp.bfloat16), inv_rms)

def norm_backward(hidden, inv_rms, norm_gain, normed_cot):
    weighted = normed_cot * norm_gain
    inner_mean = lax.optimization_barrier(jnp.mean(weighted * hidden, axis=1, keepdims=True))
    return inv_rms * weighted - inv_rms * inv_rms * inv_rms * hidden * inner_mean

def pair_slots(pair_expert, expert_count):
    onehot = (pair_expert[:, None] == jnp.arange(expert_count, dtype=jnp.int32)[None, :]).astype(jnp.int32)
    before = jnp.cumsum(onehot, axis=0) - onehot
    return (lax.optimization_barrier(jnp.sum(before * onehot, axis=1)), onehot)

def down_blocks(activated, down_w):
    count = N_DP * N_GROUP
    width = activated.shape[1] // count

    def step(total, block_id):
        left = lax.dynamic_slice_in_dim(activated, block_id * width, width, 1)
        right = lax.dynamic_slice_in_dim(down_w, block_id * width, width, 0)
        term = jnp.dot(left, right, preferred_element_type=jnp.float32).astype(jnp.bfloat16)
        term = lax.optimization_barrier(term)
        return (total + term.astype(jnp.float32), None)
    start = jnp.zeros((activated.shape[0], down_w.shape[1]), jnp.float32)
    total, _unused = lax.scan(step, start, jnp.arange(count, dtype=jnp.int32))
    return total

def input_blocks(d_gate, d_up, gate_w, up_w):
    count = N_DP * N_GROUP
    width = d_gate.shape[1] // count

    def step(total, block_id):
        gate_part = lax.dynamic_slice_in_dim(d_gate, block_id * width, width, 1)
        up_part = lax.dynamic_slice_in_dim(d_up, block_id * width, width, 1)
        gate_cols = lax.dynamic_slice_in_dim(gate_w, block_id * width, width, 1)
        up_cols = lax.dynamic_slice_in_dim(up_w, block_id * width, width, 1)
        term = (contract_cols(gate_part, gate_cols) + contract_cols(up_part, up_cols)).astype(jnp.bfloat16)
        term = lax.optimization_barrier(term)
        return (total + term.astype(jnp.float32), None)
    start = jnp.zeros((d_gate.shape[0], gate_w.shape[0]), jnp.float32)
    total, _unused = lax.scan(step, start, jnp.arange(count, dtype=jnp.int32))
    return total

def expert_forward(inputs, gate_pair, up_pair, down_pair):
    gates, ups, acts, halves = ([], [], [], [])
    for half in range(2):
        pre_gate = jnp.dot(inputs, gate_pair[half], preferred_element_type=jnp.float32)
        pre_up = jnp.dot(inputs, up_pair[half], preferred_element_type=jnp.float32)
        activated = (pre_gate * jax.nn.sigmoid(pre_gate) * pre_up).astype(jnp.bfloat16)
        half_out = down_blocks(activated, down_pair[half]).astype(jnp.bfloat16)
        gates.append(pre_gate)
        ups.append(pre_up)
        acts.append(activated)
        halves.append(half_out)
    produced = (halves[0].astype(jnp.float32) + halves[1].astype(jnp.float32)).astype(jnp.bfloat16)
    return (produced, jnp.stack(gates), jnp.stack(ups), jnp.stack(acts))

def expert_backward(out_cot, pre_gates, pre_ups, gate_pair, up_pair, down_pair):
    halves = []
    for half in range(2):
        pre_gate = pre_gates[half]
        pre_up = pre_ups[half]
        act_cot = contract_cols(out_cot, down_pair[half])
        sig_gate = jax.nn.sigmoid(pre_gate)
        d_gate = (act_cot * pre_up * sig_gate * (1.0 + pre_gate * (1.0 - sig_gate))).astype(jnp.bfloat16)
        d_up = (act_cot * pre_gate * sig_gate).astype(jnp.bfloat16)
        halves.append(input_blocks(d_gate, d_up, gate_pair[half], up_pair[half]).astype(jnp.bfloat16))
    return (halves[0].astype(jnp.float32) + halves[1].astype(jnp.float32)).astype(jnp.bfloat16)

def reference(resid, mixer_out, out_proj, norm_gain, router, routes, w_gate, w_up, w_down, cotangent):
    group_count = N_TENSOR * N_GROUP

    def add_group(running, group_id):
        part_y = lax.dynamic_slice_in_dim(mixer_out, group_id * CH, CH, 1)
        part_w = lax.dynamic_slice_in_dim(out_proj, group_id * CH, CH, 0)
        part_term = jnp.dot(part_y, part_w, preferred_element_type=jnp.float32).astype(jnp.bfloat16)
        part_term = lax.optimization_barrier(part_term)
        return (running + part_term.astype(jnp.float32), None)
    summed, _unused = lax.scan(add_group, jnp.zeros((TOKENS, D), jnp.float32), jnp.arange(group_count, dtype=jnp.int32))
    hidden = resid.astype(jnp.float32) + summed
    normed, inv_rms = norm_forward(hidden, norm_gain)
    logits = jnp.dot(normed.astype(jnp.float32), router, precision=lax.Precision.HIGHEST)
    pair_expert = routes.reshape(-1).astype(jnp.int32)
    block_count = TOKENS // TOK_DEV
    slot_pos, onehot = jax.vmap(pair_slots, in_axes=(0, None))(pair_expert.reshape(block_count, 2 * TOK_DEV), EXPERTS)
    onehot_f = onehot.reshape(2 * TOKENS, EXPERTS).astype(jnp.float32)
    pair_block = jnp.arange(2 * TOKENS, dtype=jnp.int32) // (2 * TOK_DEV)
    position = (pair_block * CAP + slot_pos.reshape(-1)).astype(jnp.int32)
    pair_logit = lax.optimization_barrier(jnp.sum(jnp.repeat(logits, 2, axis=0) * onehot_f, axis=1))
    gate_vals = jax.nn.sigmoid(pair_logit)
    pair_rows = jnp.repeat(normed, 2, axis=0)
    half_units = w_gate.shape[2]
    gate_pairs = w_gate.reshape(EXPERTS, 2, D, half_units)
    up_pairs = w_up.reshape(EXPERTS, 2, D, half_units)
    down_pairs = w_down.reshape(EXPERTS, 2, half_units, D)
    buffer = jnp.zeros((EXPERTS, block_count * CAP, D), jnp.bfloat16).at[pair_expert, position].set(pair_rows)
    produced, pre_gate, pre_up, activated = lax.map(lambda packed: expert_forward(packed[0], packed[1], packed[2], packed[3]), (buffer, gate_pairs, up_pairs, down_pairs))
    pair_out = produced[pair_expert, position]
    mixture = lax.optimization_barrier(jnp.sum((gate_vals[:, None] * pair_out.astype(jnp.float32)).reshape(TOKENS, 2, D), axis=1))
    layer_out = (hidden + mixture).astype(jnp.bfloat16)
    cot_full = cotangent.astype(jnp.float32)
    pair_cot = jnp.repeat(cot_full, 2, axis=0)
    out_cot = (gate_vals[:, None] * pair_cot).astype(jnp.bfloat16)
    gate_cot = lax.optimization_barrier(jnp.sum(pair_cot * pair_out.astype(jnp.float32), axis=1))
    cot_buffer = jnp.zeros((EXPERTS, block_count * CAP, D), jnp.bfloat16).at[pair_expert, position].set(out_cot)
    in_cot = lax.map(lambda packed: expert_backward(packed[0], packed[1], packed[2], packed[3], packed[4], packed[5]), (cot_buffer, pre_gate, pre_up, gate_pairs, up_pairs, down_pairs))
    grad_down = lax.map(lambda packed: jnp.stack([contract_rows(packed[0][0], packed[1]), contract_rows(packed[0][1], packed[1])]), (activated, cot_buffer))
    grad_down = grad_down.reshape(2 * EXPERTS, half_units, D).astype(jnp.bfloat16)
    pair_in = in_cot[pair_expert, position].astype(jnp.float32)
    normed_cot = lax.optimization_barrier(jnp.sum(pair_in.reshape(TOKENS, 2, D), axis=1))
    logit_pair = gate_cot * gate_vals * (1.0 - gate_vals)
    logit_cot = lax.optimization_barrier(jnp.sum((onehot_f * logit_pair[:, None]).reshape(TOKENS, 2, EXPERTS), axis=1))
    normed_cot = normed_cot + jnp.dot(logit_cot, router.T, precision=lax.Precision.HIGHEST)
    hidden_cot = (cot_full + norm_backward(hidden, inv_rms, norm_gain, normed_cot)).astype(jnp.bfloat16)
    grad_mixer = contract_cols(hidden_cot, out_proj).astype(jnp.bfloat16)
    return (layer_out, grad_mixer, grad_down)
```

```python
import functools

import jax
import jax.numpy as jnp
from jax import lax
from jax.experimental import pallas as pl
from jax.experimental.pallas import tpu as pltpu
from jax.sharding import PartitionSpec as P

MESH = pl.DeviceIdType.MESH
F32 = jnp.float32
BF16 = jnp.bfloat16
VMEM_MIB = 56


def contract_rows(left, right):
    return lax.dot_general(left, right, (((0,), (0,)), ((), ())), preferred_element_type=F32)


def contract_cols(left, right):
    return lax.dot_general(left, right, (((1,), (1,)), ((), ())), preferred_element_type=F32)


def norm_backward(hidden, inv_rms, norm_gain, normed_cot):
    weighted = normed_cot * norm_gain
    inner_mean = jnp.mean(weighted * hidden, axis=1, keepdims=True)
    return inv_rms * weighted - inv_rms * inv_rms * inv_rms * hidden * inner_mean


class Place:
    def __init__(self, n_dp, experts, width):
        self.n_dp, self.experts = n_dp, experts
        self.half, self.quarter, self.piece = width // 2, width // 4, width // (4 * experts)
        self.x, self.c = lax.axis_index("dp"), lax.axis_index("group")
        tensor = lax.axis_index("tensor")
        self.e, self.h = tensor // 2, lax.rem(tensor, 2)

    def device(self, x=None, e=None, h=None, c=None):
        x = self.x if x is None else x
        e = self.e if e is None else e
        h = self.h if h is None else h
        c = self.c if c is None else c
        return (x, 2 * e + h, c)

    def step_x(self, d):
        return lax.rem(self.x + (d + self.n_dp), self.n_dp)

    def step_e(self, d):
        return lax.rem(self.e + (d + self.experts), self.experts)

    def cols_c(self, c):
        return pl.ds(pl.multiple_of(c * self.half, self.half), self.half)

    def cols_h(self, h, c):
        return pl.ds(pl.multiple_of(c * self.half + h * self.quarter, self.quarter), self.quarter)

    def cols_e(self, e, h, c):
        start = c * self.half + h * self.quarter + e * self.piece
        return pl.ds(pl.multiple_of(start, self.piece), self.piece)


class Sender:
    def __init__(self, send_sems, recv_sems):
        self.send_sems, self.recv_sems, self.copies = send_sems, recv_sems, []

    def start(self, src, dst, device):
        k = len(self.copies)
        copy = pltpu.make_async_remote_copy(
            src_ref=src,
            dst_ref=dst,
            send_sem=self.send_sems.at[k],
            recv_sem=self.recv_sems.at[k],
            device_id=device,
            device_id_type=MESH,
        )
        copy.start()
        self.copies.append(copy)
        return copy

    def finish(self):
        for copy in self.copies:
            copy.wait_send()


def greet(devices):
    barrier = pltpu.get_barrier_semaphore()
    for device in devices:
        pl.semaphore_signal(barrier, inc=1, device_id=device, device_id_type=MESH)
    pl.semaphore_wait(barrier, len(devices))


def forward(place, sender, ref, where, **to):
    return sender.start(ref.at[where], ref.at[where], place.device(**to))


def gather_start(place, sender, out):
    here = place
    where = (slice(None), here.cols_e(here.e, here.h, here.c))
    return [None] + [
        forward(here, sender, out, where, e=here.step_e(d)) for d in range(1, here.experts)
    ]


def gather_rest(place, sender, started):
    here = place
    over_h, over_c = {}, []
    for d in range(here.experts):
        where = (slice(None), here.cols_e(here.step_e(-d), here.h, here.c))
        for i, (out, over_e) in enumerate(started):
            if d:
                over_e[d].wait_recv()
            over_h[i, d] = forward(here, sender, out, where, h=1 - here.h)
            over_c.append(forward(here, sender, out, where, c=1 - here.c))
    for d in range(here.experts):
        where = (slice(None), here.cols_e(here.step_e(-d), 1 - here.h, here.c))
        for i, (out, over_e) in enumerate(started):
            over_h[i, d].wait_recv()
            over_c.append(forward(here, sender, out, where, c=1 - here.c))
    for copy in over_c:
        copy.wait_recv()


def gather_and_dispatch(place, sender, over_e, hidden, select_t, rows, rows_of):
    here = place
    steps_x = range(1, here.n_dp)

    def pick(cols):
        rows[rows_of(here.x), cols] = jnp.dot(
            select_t[...], hidden[:, cols], preferred_element_type=F32
        ).astype(BF16)

    over_h, over_c, over_x, rows_h, rows_c = {}, [], {}, {}, []
    for d in range(here.experts):
        cols = here.cols_e(here.step_e(-d), here.h, here.c)
        if d:
            over_e[d].wait_recv()
        over_h[d] = forward(here, sender, hidden, (slice(None), cols), h=1 - here.h)
        over_c.append(forward(here, sender, hidden, (slice(None), cols), c=1 - here.c))
        pick(cols)
        for s in steps_x:
            over_x[d, s] = forward(
                here, sender, rows, (rows_of(here.x), cols), x=here.step_x(s)
            )
    for d in range(here.experts):
        cols = here.cols_e(here.step_e(-d), here.h, here.c)
        for s in steps_x:
            over_x[d, s].wait_recv()
            where = (rows_of(here.step_x(-s)), cols)
            rows_h[d, s] = forward(here, sender, rows, where, h=1 - here.h)
            rows_c.append(forward(here, sender, rows, where, c=1 - here.c))
        other = here.cols_e(here.step_e(-d), 1 - here.h, here.c)
        over_h[d].wait_recv()
        over_c.append(forward(here, sender, hidden, (slice(None), other), c=1 - here.c))
        pick(other)
    for d in range(here.experts):
        cols = here.cols_e(here.step_e(-d), 1 - here.h, here.c)
        for s in steps_x:
            rows_h[d, s].wait_recv()
            where = (rows_of(here.step_x(-s)), cols)
            rows_c.append(forward(here, sender, rows, where, c=1 - here.c))
    for copy in over_c:
        copy.wait_recv()
    pick(here.cols_c(1 - here.c))
    for copy in rows_c:
        copy.wait_recv()


def tiles(extent, most):
    size = 128
    while size * 2 <= most and extent % (size * 2) == 0:
        size *= 2
    return size, extent // size


def layer_kernel(
    n_dp,
    experts,
    own_ref,
    cots_ref,
    select_ref,
    select_t,
    resid_ref,
    gain_ref,
    router_ref,
    gate_hbm,
    up_hbm,
    down_hbm,
    hidden_ref,
    mix_ref,
    cot_ref,
    act_ref,
    out_cot_ref,
    w_gate,
    w_up,
    w_down,
    slot_cot,
    rows,
    own_out,
    own_in,
    swap_in,
    swapped,
    hidden_parts,
    pair_in,
    paired,
    parts,
    tokens,
    pieces,
    d_gate,
    d_up,
    raw_cot,
    pre_gate,
    pre_up,
    gates,
    slopes,
    load_sems,
    send_sems,
    recv_sems,
):
    width = own_ref.shape[1]
    capacity = cots_ref.shape[0]
    slots = n_dp * capacity
    here = Place(n_dp, experts, width)
    sender = Sender(send_sems, recv_sems)
    tensor = 2 * experts
    mine = 2 * here.e + here.h

    def rows_of(x):
        return pl.ds(pl.multiple_of(x * capacity, capacity), capacity)

    loads = [
        pltpu.make_async_copy(src, dst, load_sems.at[k])
        for k, (src, dst) in enumerate(((down_hbm, w_down), (gate_hbm, w_gate), (up_hbm, w_up)))
    ]
    for load in loads:
        load.start()

    peers = []
    for d in range(1, tensor):
        other = lax.rem(mine + d, tensor)
        peers.append((other // 2, lax.rem(other, 2)))
    plane = [(d, flip) for flip in (1, 0) for d in range(n_dp)]
    devices = [here.device(c=1 - here.c)]
    devices += [here.device(e=e, h=h) for e, h in peers]
    devices += [
        here.device(x=here.step_x(d), h=lax.rem(here.h + flip, 2)) for d, flip in plane if d
    ]
    greet(devices)

    swap = sender.start(own_ref.at[:, here.cols_c(1 - here.c)], swap_in, here.device(c=1 - here.c))
    half_cols = here.cols_c(here.c)
    replicas = [
        sender.start(
            cots_ref.at[:, half_cols],
            slot_cot.at[rows_of(here.x), half_cols],
            here.device(x=here.step_x(d)),
        )
        for d in range(1, n_dp)
    ]
    swap.wait_recv()
    swapped[...] = (own_ref[:, half_cols].astype(F32) + swap_in[...].astype(F32)).astype(BF16)
    arrivals = [
        sender.start(swapped.at[:, here.cols_e(e, h, 0)], hidden_parts.at[d], here.device(e=e, h=h))
        for d, (e, h) in enumerate(peers)
    ]
    slot_cot[rows_of(here.x), :] = cots_ref[...]
    shared = []
    for d in range(1, n_dp):
        replicas[d - 1].wait_recv()
        where = (rows_of(here.step_x(-d)), half_cols)
        shared.append(forward(here, sender, slot_cot, where, c=1 - here.c))
    own_cols = here.cols_e(here.e, here.h, here.c)
    total = swapped[:, here.cols_e(here.e, here.h, 0)].astype(F32)
    total = total + resid_ref[:, own_cols].astype(F32)
    for d, copy in enumerate(arrivals):
        copy.wait_recv()
        total = total + hidden_parts[d].astype(F32)
    hidden_ref[:, own_cols] = total.astype(BF16)
    over_e = gather_start(here, sender, hidden_ref)

    for copy in shared:
        copy.wait_recv()
    loads[0].wait()
    depth, steps = tiles(width, 1024)
    raw_cot[...] = jnp.zeros_like(raw_cot)

    @pl.loop(0, steps)
    def _(k):
        cols = pl.ds(pl.multiple_of(k * depth, depth), depth)
        raw_cot[...] += contract_cols(slot_cot[:, cols], w_down[:, cols])

    gather_and_dispatch(here, sender, over_e, hidden_ref, select_t, rows, rows_of)

    @pl.loop(0, slots // 16)
    def _(k):
        block = pl.ds(pl.multiple_of(k * 16, 16), 16)
        value = rows[block, :].astype(F32)
        inv_rms = lax.rsqrt(jnp.mean(value * value, axis=1, keepdims=True) + 1e-05)
        normed = (value * inv_rms * gain_ref[...]).astype(BF16)
        own_in[block, :] = normed
        logit = jnp.sum(normed.astype(F32) * router_ref[...], axis=1, keepdims=True)
        gate = jax.nn.sigmoid(logit)
        gates[block, :] = gate
        out_cot_ref[block, :] = (gate * slot_cot[block, :].astype(F32)).astype(BF16)

    loads[1].wait()
    loads[2].wait()
    pre_gate[...] = jnp.zeros_like(pre_gate)
    pre_up[...] = jnp.zeros_like(pre_up)

    @pl.loop(0, steps)
    def _(k):
        cols = pl.ds(pl.multiple_of(k * depth, depth), depth)
        pre_gate[...] += jnp.dot(own_in[:, cols], w_gate[cols, :], preferred_element_type=F32)
        pre_up[...] += jnp.dot(own_in[:, cols], w_up[cols, :], preferred_element_type=F32)

    @pl.loop(0, slots // 16)
    def _(k):
        block = pl.ds(pl.multiple_of(k * 16, 16), 16)
        gate, raw = gates[block, :], raw_cot[block, :]
        z, up = pre_gate[block, :], pre_up[block, :]
        sig = jax.nn.sigmoid(z)
        act = (z * sig * up).astype(BF16)
        act_ref[block, :] = act
        act_cot = gate * raw
        d_gate[block, :] = (act_cot * up * sig * (1.0 + z * (1.0 - sig))).astype(BF16)
        d_up[block, :] = (act_cot * z * sig).astype(BF16)
        gate_cot = jnp.sum(act.astype(F32) * raw, axis=1, keepdims=True)
        slopes[block, :] = gate_cot * gate * (1.0 - gate)

    span, spans = tiles(here.quarter, 512)

    def forward_tile(cols):
        own_out[:, cols] = (
            gates[...] * jnp.dot(act_ref[...], w_down[:, cols], preferred_element_type=F32)
        ).astype(BF16)

    def backward_tile(cols):
        own_in[:, cols] = (
            contract_cols(d_gate[...], w_gate[cols, :])
            + contract_cols(d_up[...], w_up[cols, :])
            + slopes[...] * router_ref[:, cols]
        ).astype(BF16)

    crossing = {}
    for i, (source, tile) in enumerate(((own_out, forward_tile), (own_in, backward_tile))):

        def fill(h, c, tile=tile):
            first = c * here.half + h * here.quarter

            @pl.loop(0, spans)
            def _(k):
                tile(pl.ds(pl.multiple_of(first + k * span, span), span))

        swaps = {}
        for flip in (1, 0):
            h = lax.rem(here.h + flip, 2)
            fill(h, 1 - here.c)
            for k, (d, f) in enumerate(plane):
                if f == flip:
                    swaps[k] = sender.start(
                        source.at[rows_of(here.step_x(d)), here.cols_h(h, 1 - here.c)],
                        pair_in.at[i, k],
                        here.device(c=1 - here.c),
                    )
        for flip in (1, 0):
            h = lax.rem(here.h + flip, 2)
            fill(h, here.c)
            for k, (d, f) in enumerate(plane):
                if f == flip:
                    swaps[k].wait_recv()
                    paired[i, k] = (
                        source[rows_of(here.step_x(d)), here.cols_h(h, here.c)].astype(F32)
                        + pair_in[i, k].astype(F32)
                    ).astype(BF16)
                    if d or f:
                        crossing[i, k] = sender.start(
                            paired.at[i, k], parts.at[i, k], here.device(x=here.step_x(d), h=h)
                        )

    own_slot = plane.index((0, 0))
    scattered = {}
    for i in range(2):
        total = paired[i, own_slot].astype(F32)
        for k in range(len(plane)):
            if k != own_slot:
                crossing[i, k].wait_recv()
                total = total + parts[i, k].astype(F32)
        tokens[i] = jnp.dot(
            select_ref[...], total.astype(BF16), preferred_element_type=F32
        ).astype(BF16)
        for d in range(1, experts):
            e = here.step_e(d)
            cols = pl.ds(pl.multiple_of(e * here.piece, here.piece), here.piece)
            scattered[i, d] = sender.start(
                tokens.at[i, :, cols], pieces.at[i, d - 1], here.device(e=e)
            )
    mine_cols = pl.ds(pl.multiple_of(here.e * here.piece, here.piece), here.piece)
    started = []
    for i, result in enumerate((mix_ref, cot_ref)):
        total = tokens[i, :, mine_cols].astype(F32)
        for d in range(1, experts):
            scattered[i, d].wait_recv()
            total = total + pieces[i, d - 1].astype(F32)
        result[:, own_cols] = total.astype(BF16)
        started.append((result, gather_start(here, sender, result)))
    gather_rest(here, sender, started)
    sender.finish()


def on_device(
    n_dp, resid, mixer_out, out_proj, norm_gain, router, routes, w_gate, w_up, w_down, cotangent
):
    row_count, width = resid.shape
    experts = router.shape[1]
    capacity = min(row_count, 3 * row_count // experts)
    half, quarter, piece = width // 2, width // 4, width // (4 * experts)
    expert_id = lax.axis_index("tensor") // 2

    hit = jnp.any(routes == expert_id, axis=1)
    earlier = jnp.arange(row_count)[None, :] < jnp.arange(row_count)[:, None]
    slot_pos = jnp.sum((earlier & hit[None, :]).astype(jnp.int32), axis=1)
    select = (
        hit[:, None] & (slot_pos[:, None] == jnp.arange(capacity, dtype=jnp.int32)[None, :])
    ).astype(BF16)
    local_cots = contract_rows(select, cotangent).astype(BF16)

    own_term = jnp.dot(mixer_out, out_proj, preferred_element_type=F32).astype(BF16)
    slots, units, plane = n_dp * capacity, w_gate.shape[2], 2 * n_dp
    router_row = lax.dynamic_slice_in_dim(router, expert_id, 1, 1).T
    gathers = 4 * experts - 1
    dispatch = 4 * experts * (n_dp - 1)
    reduce = 1 + 2 * (n_dp - 1) + 2 * experts - 1
    combine = 2 * (plane + plane - 1 + experts - 1 + gathers)
    copies = reduce + gathers + dispatch + combine
    whole = pl.BlockSpec(memory_space=pltpu.VMEM)
    remote = pl.BlockSpec(memory_space=pl.ANY)
    hidden_bf, mixture, normed_cot, activated, out_cot = pl.pallas_call(
        functools.partial(layer_kernel, n_dp, experts),
        out_shape=[jax.ShapeDtypeStruct((row_count, width), BF16)] * 3
        + [
            jax.ShapeDtypeStruct((slots, units), BF16),
            jax.ShapeDtypeStruct((slots, width), BF16),
        ],
        in_specs=[whole] * 7 + [remote] * 3,
        out_specs=[whole] * 5,
        scratch_shapes=[
            pltpu.VMEM((width, units), BF16),
            pltpu.VMEM((width, units), BF16),
            pltpu.VMEM((units, width), BF16),
            pltpu.VMEM((slots, width), BF16),
            pltpu.VMEM((slots, width), BF16),
            pltpu.VMEM((slots, width), BF16),
            pltpu.VMEM((slots, width), BF16),
            pltpu.VMEM((row_count, half), BF16),
            pltpu.VMEM((row_count, half), BF16),
            pltpu.VMEM((2 * experts - 1, row_count, piece), BF16),
            pltpu.VMEM((2, plane, capacity, quarter), BF16),
            pltpu.VMEM((2, plane, capacity, quarter), BF16),
            pltpu.VMEM((2, plane, capacity, quarter), BF16),
            pltpu.VMEM((2, row_count, quarter), BF16),
            pltpu.VMEM((2, experts - 1, row_count, piece), BF16),
            pltpu.VMEM((slots, units), BF16),
            pltpu.VMEM((slots, units), BF16),
            pltpu.VMEM((slots, units), F32),
            pltpu.VMEM((slots, units), F32),
            pltpu.VMEM((slots, units), F32),
            pltpu.VMEM((slots, 1), F32),
            pltpu.VMEM((slots, 1), F32),
            pltpu.SemaphoreType.DMA((3,)),
            pltpu.SemaphoreType.DMA((copies,)),
            pltpu.SemaphoreType.DMA((copies,)),
        ],
        compiler_params=pltpu.CompilerParams(
            collective_id=0, has_side_effects=True, vmem_limit_bytes=VMEM_MIB * 1024 * 1024
        ),
    )(
        own_term,
        local_cots,
        select,
        select.T,
        resid,
        norm_gain[None],
        router_row,
        w_gate[0],
        w_up[0],
        w_down[0],
    )
    grad_down = contract_rows(activated, out_cot).astype(BF16)[None]
    hidden = hidden_bf.astype(F32)
    inv_rms = lax.rsqrt(jnp.mean(hidden * hidden, axis=1, keepdims=True) + 1e-05)
    layer_out = (hidden + mixture.astype(F32)).astype(BF16)
    hidden_cot = (
        cotangent.astype(F32)
        + norm_backward(hidden, inv_rms, norm_gain, normed_cot.astype(F32))
    ).astype(BF16)
    grad_mixer = contract_cols(hidden_cot, out_proj).astype(BF16)
    return (layer_out, grad_mixer, grad_down)


def solution(mesh):
    placed = (
        P("dp", None),
        P("dp", ("tensor", "group")),
        P(("tensor", "group"), None),
        P(),
        P(),
        P("dp", None),
        P("tensor", None, ("dp", "group")),
        P("tensor", None, ("dp", "group")),
        P("tensor", ("dp", "group"), None),
        P("dp", None),
    )
    return jax.shard_map(
        functools.partial(on_device, mesh.shape["dp"]),
        mesh=mesh,
        in_specs=placed,
        out_specs=(P("dp", None), P("dp", ("tensor", "group")), P("tensor", ("dp", "group"), None)),
        check_vma=False,
    )
```

```python
import functools

import jax
import jax.numpy as jnp
from jax import lax
from jax.experimental import pallas as pl
from jax.experimental.pallas import tpu as pltpu
from jax.sharding import PartitionSpec as P

MESH = pl.DeviceIdType.MESH
F32 = jnp.float32
BF16 = jnp.bfloat16
VMEM_MIB = 60


def contract_rows(left, right):
    return lax.dot_general(left, right, (((0,), (0,)), ((), ())), preferred_element_type=F32)


def contract_cols(left, right):
    return lax.dot_general(left, right, (((1,), (1,)), ((), ())), preferred_element_type=F32)


class Place:
    def __init__(self, n_dp, experts, width):
        self.n_dp, self.experts = n_dp, experts
        self.half, self.quarter, self.piece = width // 2, width // 4, width // (4 * experts)
        self.x, self.c = lax.axis_index("dp"), lax.axis_index("group")
        tensor = lax.axis_index("tensor")
        self.e, self.h = tensor // 2, lax.rem(tensor, 2)

    def device(self, x=None, e=None, h=None, c=None):
        x = self.x if x is None else x
        e = self.e if e is None else e
        h = self.h if h is None else h
        c = self.c if c is None else c
        return (x, 2 * e + h, c)

    def step_x(self, d):
        return lax.rem(self.x + (d + self.n_dp), self.n_dp)

    def step_e(self, d):
        return lax.rem(self.e + (d + self.experts), self.experts)

    def cols_c(self, c):
        return pl.ds(pl.multiple_of(c * self.half, self.half), self.half)

    def cols_h(self, h, c):
        return pl.ds(pl.multiple_of(c * self.half + h * self.quarter, self.quarter), self.quarter)

    def cols_e(self, e, h, c):
        start = c * self.half + h * self.quarter + e * self.piece
        return pl.ds(pl.multiple_of(start, self.piece), self.piece)


class Sender:
    def __init__(self, send_sems, recv_sems):
        self.send_sems, self.recv_sems, self.copies = send_sems, recv_sems, []

    def start(self, src, dst, device):
        k = len(self.copies)
        copy = pltpu.make_async_remote_copy(
            src_ref=src,
            dst_ref=dst,
            send_sem=self.send_sems.at[k],
            recv_sem=self.recv_sems.at[k],
            device_id=device,
            device_id_type=MESH,
        )
        copy.start()
        self.copies.append(copy)
        return copy

    def finish(self):
        for copy in self.copies:
            copy.wait_send()


def greet(devices):
    barrier = pltpu.get_barrier_semaphore()
    for device in devices:
        pl.semaphore_signal(barrier, inc=1, device_id=device, device_id_type=MESH)
    pl.semaphore_wait(barrier, len(devices))


def forward(place, sender, ref, where, **to):
    return sender.start(ref.at[where], ref.at[where], place.device(**to))


def gather_start(place, sender, out):
    here = place
    where = (slice(None), here.cols_e(here.e, here.h, here.c))
    return [None] + [
        forward(here, sender, out, where, e=here.step_e(d)) for d in range(1, here.experts)
    ]


def gather_pass(place, sender, out, over_e):
    here = place
    over_h, over_c = [], []
    for d in range(here.experts):
        where = (slice(None), here.cols_e(here.step_e(-d), here.h, here.c))
        if d:
            over_e[d].wait_recv()
        over_h.append(forward(here, sender, out, where, h=1 - here.h))
        over_c.append(forward(here, sender, out, where, c=1 - here.c))
    return over_h, over_c


def gather_finish(place, sender, out, over_h, over_c):
    here = place
    for d in range(here.experts):
        where = (slice(None), here.cols_e(here.step_e(-d), 1 - here.h, here.c))
        over_h[d].wait_recv()
        over_c.append(forward(here, sender, out, where, c=1 - here.c))
    for copy in over_c:
        copy.wait_recv()


def gather_and_dispatch(place, sender, over_e, hidden, select_t, rows, rows_of):
    here = place
    steps_x = range(1, here.n_dp)

    def pick(cols):
        rows[rows_of(here.x), cols] = jnp.dot(
            select_t[...], hidden[:, cols], preferred_element_type=F32
        ).astype(BF16)

    over_h, over_c, over_x, rows_h, rows_c = {}, [], {}, {}, []
    for d in range(here.experts):
        cols = here.cols_e(here.step_e(-d), here.h, here.c)
        if d:
            over_e[d].wait_recv()
        over_h[d] = forward(here, sender, hidden, (slice(None), cols), h=1 - here.h)
        over_c.append(forward(here, sender, hidden, (slice(None), cols), c=1 - here.c))
        pick(cols)
        for s in steps_x:
            over_x[d, s] = forward(
                here, sender, rows, (rows_of(here.x), cols), x=here.step_x(s)
            )
    for d in range(here.experts):
        cols = here.cols_e(here.step_e(-d), here.h, here.c)
        for s in steps_x:
            over_x[d, s].wait_recv()
            where = (rows_of(here.step_x(-s)), cols)
            rows_h[d, s] = forward(here, sender, rows, where, h=1 - here.h)
            rows_c.append(forward(here, sender, rows, where, c=1 - here.c))
        other = here.cols_e(here.step_e(-d), 1 - here.h, here.c)
        over_h[d].wait_recv()
        over_c.append(forward(here, sender, hidden, (slice(None), other), c=1 - here.c))
        pick(other)
    for d in range(here.experts):
        cols = here.cols_e(here.step_e(-d), 1 - here.h, here.c)
        for s in steps_x:
            rows_h[d, s].wait_recv()
            where = (rows_of(here.step_x(-s)), cols)
            rows_c.append(forward(here, sender, rows, where, c=1 - here.c))
    for copy in over_c:
        copy.wait_recv()
    pick(here.cols_c(1 - here.c))
    return rows_c


def tiles(extent, most):
    size = 128
    while size * 2 <= most and extent % (size * 2) == 0:
        size *= 2
    return size, extent // size


def layer_kernel(
    n_dp,
    experts,
    mixer_ref,
    routes_ref,
    routes_t,
    cotangent_ref,
    resid_ref,
    gain_ref,
    router_ref,
    gate_hbm,
    up_hbm,
    down_hbm,
    proj_hbm,
    layer_ref,
    mixer_cot_ref,
    act_ref,
    out_cot_ref,
    w_gate,
    w_up,
    w_down,
    w_proj,
    own,
    hidden,
    mix,
    cot,
    select,
    select_t,
    slot_cot,
    rows,
    own_out,
    own_in,
    swap_in,
    swapped,
    half_in,
    half_sum,
    hidden_parts,
    pair_in,
    paired,
    parts,
    tokens,
    pieces,
    d_gate,
    d_up,
    raw_cot,
    pre_gate,
    pre_up,
    gates,
    slopes,
    hidden_cot,
    load_sems,
    send_sems,
    recv_sems,
):
    row_count, width = resid_ref.shape
    slots = slot_cot.shape[0]
    capacity = slots // n_dp
    here = Place(n_dp, experts, width)
    sender = Sender(send_sems, recv_sems)

    def rows_of(x):
        return pl.ds(pl.multiple_of(x * capacity, capacity), capacity)

    loads = [
        pltpu.make_async_copy(src, dst, load_sems.at[k])
        for k, (src, dst) in enumerate(((down_hbm, w_down), (gate_hbm, w_gate), (up_hbm, w_up)))
    ]
    blocks = [(flip, other) for other in (1, 0) for flip in (1, 0)]
    proj_loads = []
    for k, (flip, other) in enumerate(blocks):
        cols = here.cols_h(lax.rem(here.h + flip, 2), lax.rem(here.c + other, 2))
        load = pltpu.make_async_copy(
            proj_hbm.at[:, cols], w_proj.at[:, cols], load_sems.at[3 + k]
        )
        load.start()
        proj_loads.append((cols, load))

    plane = [(d, flip) for flip in (1, 0) for d in range(n_dp)]
    devices = [here.device(c=1 - here.c)]
    devices += [here.device(e=here.step_e(d)) for d in range(1, experts)]
    devices += [
        here.device(x=here.step_x(d), h=lax.rem(here.h + flip, 2)) for d, flip in plane if d or flip
    ]
    greet(devices)

    hit = ((routes_ref[:, 0:1] == here.e) | (routes_ref[:, 1:2] == here.e)).astype(F32)
    hit_t = ((routes_t[0:1, :] == here.e) | (routes_t[1:2, :] == here.e)).astype(F32)
    row = lax.broadcasted_iota(jnp.int32, (row_count, row_count), 0)
    col = lax.broadcasted_iota(jnp.int32, (row_count, row_count), 1)
    slot = jnp.sum(jnp.where(col < row, hit_t, 0.0), axis=1, keepdims=True)
    slot_t = jnp.sum(jnp.where(row < col, hit, 0.0), axis=0, keepdims=True)
    number = lax.broadcasted_iota(jnp.int32, (row_count, capacity), 1).astype(F32)
    number_t = lax.broadcasted_iota(jnp.int32, (capacity, row_count), 0).astype(F32)
    select[...] = jnp.where(slot == number, hit, 0.0).astype(BF16)
    select_t[...] = jnp.where(slot_t == number_t, hit_t, 0.0).astype(BF16)

    half_cols = here.cols_c(here.c)
    own_rows = rows_of(here.x)

    def pick_cot(cols):
        slot_cot[own_rows, cols] = jnp.dot(
            select_t[...], cotangent_ref[:, cols], preferred_element_type=F32
        ).astype(BF16)

    pick_cot(half_cols)
    replicas = [
        forward(here, sender, slot_cot, (own_rows, half_cols), x=here.step_x(d))
        for d in range(1, n_dp)
    ]

    swaps = []
    for (flip, other), (cols, load) in zip(blocks, proj_loads):
        load.wait()
        own[:, cols] = jnp.dot(
            mixer_ref[...], w_proj[:, cols], preferred_element_type=F32
        ).astype(BF16)
        if other:
            there = here.cols_h(lax.rem(here.h + flip, 2), 0)
            swaps.append(
                sender.start(own.at[:, cols], swap_in.at[:, there], here.device(c=1 - here.c))
            )
    for load in loads:
        load.start()
    order = list(range(1, experts)) + [0]
    halves = {}
    for flip in (1, 0):
        h = lax.rem(here.h + flip, 2)
        there = here.cols_h(h, 0)
        swaps[1 - flip].wait_recv()
        swapped[:, there] = (
            own[:, here.cols_h(h, here.c)].astype(F32) + swap_in[:, there].astype(F32)
        ).astype(BF16)
        if flip:
            for d in order:
                halves[d] = sender.start(
                    swapped.at[:, here.cols_e(here.step_e(d), h, 0)],
                    half_in.at[d],
                    here.device(h=h),
                )
    pick_cot(here.cols_c(1 - here.c))
    arrivals = {}
    for d in order:
        halves[d].wait_recv()
        total = swapped[:, here.cols_e(here.step_e(d), here.h, 0)].astype(F32)
        total = total + half_in[d].astype(F32)
        if d:
            half_sum[d - 1] = total.astype(BF16)
            arrivals[d] = sender.start(
                half_sum.at[d - 1], hidden_parts.at[d - 1], here.device(e=here.step_e(d))
            )
    shared = []
    for d in range(1, n_dp):
        replicas[d - 1].wait_recv()
        where = (rows_of(here.step_x(-d)), half_cols)
        shared.append(forward(here, sender, slot_cot, where, c=1 - here.c))
    own_cols = here.cols_e(here.e, here.h, here.c)
    total = total + resid_ref[:, own_cols].astype(F32)
    for d in range(1, experts):
        arrivals[d].wait_recv()
        total = total + hidden_parts[d - 1].astype(F32)
    hidden[:, own_cols] = total.astype(BF16)
    over_e = gather_start(here, sender, hidden)

    for copy in shared:
        copy.wait_recv()
    loads[0].wait()
    depth, steps = tiles(width, 1024)
    raw_cot[...] = jnp.zeros_like(raw_cot)

    @pl.loop(0, steps)
    def _(k):
        cols = pl.ds(pl.multiple_of(k * depth, depth), depth)
        raw_cot[...] += contract_cols(slot_cot[:, cols], w_down[:, cols])

    router_row = router_ref.at[pl.ds(here.e, 1), :]
    rows_c = gather_and_dispatch(here, sender, over_e, hidden, select_t, rows, rows_of)

    def norm_rows(x):
        @pl.loop(0, capacity // 16)
        def _(k):
            block = pl.ds(pl.multiple_of(x * capacity + k * 16, 16), 16)
            value = rows[block, :].astype(F32)
            inv_rms = lax.rsqrt(jnp.mean(value * value, axis=1, keepdims=True) + 1e-05)
            normed = (value * inv_rms * gain_ref[...]).astype(BF16)
            own_in[block, :] = normed
            logit = jnp.sum(normed.astype(F32) * router_row[...], axis=1, keepdims=True)
            gate = jax.nn.sigmoid(logit)
            gates[block, :] = gate
            out_cot_ref[block, :] = (gate * slot_cot[block, :].astype(F32)).astype(BF16)

    norm_rows(here.x)
    for copy in rows_c:
        copy.wait_recv()
    for d in range(1, n_dp):
        norm_rows(here.step_x(d))

    loads[1].wait()
    loads[2].wait()
    pre_gate[...] = jnp.zeros_like(pre_gate)
    pre_up[...] = jnp.zeros_like(pre_up)

    @pl.loop(0, steps)
    def _(k):
        cols = pl.ds(pl.multiple_of(k * depth, depth), depth)
        pre_gate[...] += jnp.dot(own_in[:, cols], w_gate[cols, :], preferred_element_type=F32)
        pre_up[...] += jnp.dot(own_in[:, cols], w_up[cols, :], preferred_element_type=F32)

    @pl.loop(0, slots // 16)
    def _(k):
        block = pl.ds(pl.multiple_of(k * 16, 16), 16)
        gate, raw = gates[block, :], raw_cot[block, :]
        z, up = pre_gate[block, :], pre_up[block, :]
        sig = jax.nn.sigmoid(z)
        act = (z * sig * up).astype(BF16)
        act_ref[block, :] = act
        act_cot = gate * raw
        d_gate[block, :] = (act_cot * up * sig * (1.0 + z * (1.0 - sig))).astype(BF16)
        d_up[block, :] = (act_cot * z * sig).astype(BF16)
        gate_cot = jnp.sum(act.astype(F32) * raw, axis=1, keepdims=True)
        slopes[block, :] = gate_cot * gate * (1.0 - gate)

    span, spans = tiles(here.quarter, 512)

    def forward_tile(cols):
        own_out[:, cols] = (
            gates[...] * jnp.dot(act_ref[...], w_down[:, cols], preferred_element_type=F32)
        ).astype(BF16)

    def backward_tile(cols):
        own_in[:, cols] = (
            contract_cols(d_gate[...], w_gate[cols, :])
            + contract_cols(d_up[...], w_up[cols, :])
            + slopes[...] * router_row[:, cols]
        ).astype(BF16)

    crossing = {}
    for i, (source, tile) in enumerate(((own_out, forward_tile), (own_in, backward_tile))):

        def fill(h, c, tile=tile):
            first = c * here.half + h * here.quarter

            @pl.loop(0, spans)
            def _(k):
                tile(pl.ds(pl.multiple_of(first + k * span, span), span))

        swaps = {}
        for flip in (1, 0):
            h = lax.rem(here.h + flip, 2)
            fill(h, 1 - here.c)
            for k, (d, f) in enumerate(plane):
                if f == flip:
                    swaps[k] = sender.start(
                        source.at[rows_of(here.step_x(d)), here.cols_h(h, 1 - here.c)],
                        pair_in.at[i, k],
                        here.device(c=1 - here.c),
                    )
        for flip in (1, 0):
            h = lax.rem(here.h + flip, 2)
            fill(h, here.c)
            for k, (d, f) in enumerate(plane):
                if f == flip:
                    swaps[k].wait_recv()
                    paired[i, k] = (
                        source[rows_of(here.step_x(d)), here.cols_h(h, here.c)].astype(F32)
                        + pair_in[i, k].astype(F32)
                    ).astype(BF16)
                    if d or f:
                        crossing[i, k] = sender.start(
                            paired.at[i, k], parts.at[i, k], here.device(x=here.step_x(d), h=h)
                        )

    own_slot = plane.index((0, 0))
    mine_cols = pl.ds(pl.multiple_of(here.e * here.piece, here.piece), here.piece)
    started = []
    for i, result in enumerate((mix, cot)):
        total = paired[i, own_slot].astype(F32)
        for k in range(len(plane)):
            if k != own_slot:
                crossing[i, k].wait_recv()
                total = total + parts[i, k].astype(F32)
        tokens[i] = jnp.dot(select[...], total.astype(BF16), preferred_element_type=F32).astype(
            BF16
        )
        scattered = []
        for d in range(1, experts):
            e = here.step_e(d)
            cols = pl.ds(pl.multiple_of(e * here.piece, here.piece), here.piece)
            scattered.append(
                sender.start(tokens.at[i, :, cols], pieces.at[i, d - 1], here.device(e=e))
            )
        if i:
            mix_passed = gather_pass(here, sender, mix, started[0])
        total = tokens[i, :, mine_cols].astype(F32)
        for d in range(1, experts):
            scattered[d - 1].wait_recv()
            total = total + pieces[i, d - 1].astype(F32)
        result[:, own_cols] = total.astype(BF16)
        started.append(gather_start(here, sender, result))
    cot_passed = gather_pass(here, sender, cot, started[1])
    gather_finish(here, sender, mix, *mix_passed)

    @pl.loop(0, row_count // 16)
    def _(k):
        block = pl.ds(pl.multiple_of(k * 16, 16), 16)
        layer_ref[block, :] = (hidden[block, :].astype(F32) + mix[block, :].astype(F32)).astype(
            BF16
        )

    gather_finish(here, sender, cot, *cot_passed)

    @pl.loop(0, row_count // 16)
    def _(k):
        block = pl.ds(pl.multiple_of(k * 16, 16), 16)
        value = hidden[block, :].astype(F32)
        inv_rms = lax.rsqrt(jnp.mean(value * value, axis=1, keepdims=True) + 1e-05)
        weighted = cot[block, :].astype(F32) * gain_ref[...]
        inner_mean = jnp.mean(weighted * value, axis=1, keepdims=True)
        change = inv_rms * weighted - inv_rms * inv_rms * inv_rms * value * inner_mean
        hidden_cot[block, :] = (cotangent_ref[block, :].astype(F32) + change).astype(BF16)

    mixer_cot_ref[...] = contract_cols(hidden_cot[...], w_proj[...]).astype(BF16)
    sender.finish()


def on_device(
    n_dp, resid, mixer_out, out_proj, norm_gain, router, routes, w_gate, w_up, w_down, cotangent
):
    row_count, width = resid.shape
    experts = router.shape[1]
    capacity = min(row_count, 3 * row_count // experts)
    half, quarter, piece = width // 2, width // 4, width // (4 * experts)
    slots, units, plane = n_dp * capacity, w_gate.shape[2], 2 * n_dp
    gathers = 4 * experts - 1
    dispatch = 4 * experts * (n_dp - 1)
    reduce = 2 + 2 * (n_dp - 1) + 2 * experts - 1
    combine = 2 * (plane + plane - 1 + experts - 1 + gathers)
    copies = reduce + gathers + dispatch + combine
    whole = pl.BlockSpec(memory_space=pltpu.VMEM)
    remote = pl.BlockSpec(memory_space=pl.ANY)
    layer_out, grad_mixer, activated, out_cot = pl.pallas_call(
        functools.partial(layer_kernel, n_dp, experts),
        out_shape=[
            jax.ShapeDtypeStruct((row_count, width), BF16),
            jax.ShapeDtypeStruct(mixer_out.shape, BF16),
            jax.ShapeDtypeStruct((slots, units), BF16),
            jax.ShapeDtypeStruct((slots, width), BF16),
        ],
        in_specs=[whole] * 7 + [remote] * 4,
        out_specs=[whole] * 4,
        scratch_shapes=[
            pltpu.VMEM((width, units), BF16),
            pltpu.VMEM((width, units), BF16),
            pltpu.VMEM((units, width), BF16),
            pltpu.VMEM(out_proj.shape, BF16),
            pltpu.VMEM((row_count, width), BF16),
            pltpu.VMEM((row_count, width), BF16),
            pltpu.VMEM((row_count, width), BF16),
            pltpu.VMEM((row_count, width), BF16),
            pltpu.VMEM((row_count, capacity), BF16),
            pltpu.VMEM((capacity, row_count), BF16),
            pltpu.VMEM((slots, width), BF16),
            pltpu.VMEM((slots, width), BF16),
            pltpu.VMEM((slots, width), BF16),
            pltpu.VMEM((slots, width), BF16),
            pltpu.VMEM((row_count, half), BF16),
            pltpu.VMEM((row_count, half), BF16),
            pltpu.VMEM((experts, row_count, piece), BF16),
            pltpu.VMEM((experts - 1, row_count, piece), BF16),
            pltpu.VMEM((experts - 1, row_count, piece), BF16),
            pltpu.VMEM((2, plane, capacity, quarter), BF16),
            pltpu.VMEM((2, plane, capacity, quarter), BF16),
            pltpu.VMEM((2, plane, capacity, quarter), BF16),
            pltpu.VMEM((2, row_count, quarter), BF16),
            pltpu.VMEM((2, experts - 1, row_count, piece), BF16),
            pltpu.VMEM((slots, units), BF16),
            pltpu.VMEM((slots, units), BF16),
            pltpu.VMEM((slots, units), F32),
            pltpu.VMEM((slots, units), F32),
            pltpu.VMEM((slots, units), F32),
            pltpu.VMEM((slots, 1), F32),
            pltpu.VMEM((slots, 1), F32),
            pltpu.VMEM((row_count, width), BF16),
            pltpu.SemaphoreType.DMA((7,)),
            pltpu.SemaphoreType.DMA((copies,)),
            pltpu.SemaphoreType.DMA((copies,)),
        ],
        compiler_params=pltpu.CompilerParams(
            collective_id=0, has_side_effects=True, vmem_limit_bytes=VMEM_MIB * 1024 * 1024
        ),
    )(
        mixer_out,
        routes,
        routes.T,
        cotangent,
        resid,
        norm_gain[None],
        router.T,
        w_gate[0],
        w_up[0],
        w_down[0],
        out_proj,
    )
    grad_down = contract_rows(activated, out_cot).astype(BF16)[None]
    return (layer_out, grad_mixer, grad_down)


def solution(mesh):
    placed = (
        P("dp", None),
        P("dp", ("tensor", "group")),
        P(("tensor", "group"), None),
        P(),
        P(),
        P("dp", None),
        P("tensor", None, ("dp", "group")),
        P("tensor", None, ("dp", "group")),
        P("tensor", ("dp", "group"), None),
        P("dp", None),
    )
    return jax.shard_map(
        functools.partial(on_device, mesh.shape["dp"]),
        mesh=mesh,
        in_specs=placed,
        out_specs=(P("dp", None), P("dp", ("tensor", "group")), P("tensor", ("dp", "group"), None)),
        check_vma=False,
    )
```

```python
import functools

import jax
import jax.numpy as jnp
from jax import lax
from jax.experimental import pallas as pl
from jax.experimental.pallas import tpu as pltpu
from jax.sharding import PartitionSpec as P

MESH = pl.DeviceIdType.MESH
F32 = jnp.float32
BF16 = jnp.bfloat16
VMEM_MIB = 60


def contract_rows(left, right):
    return lax.dot_general(left, right, (((0,), (0,)), ((), ())), preferred_element_type=F32)


def contract_cols(left, right):
    return lax.dot_general(left, right, (((1,), (1,)), ((), ())), preferred_element_type=F32)


class Place:
    def __init__(self, n_dp, experts, width):
        self.n_dp, self.experts = n_dp, experts
        self.half, self.quarter, self.piece = width // 2, width // 4, width // (4 * experts)
        self.x, self.c = lax.axis_index("dp"), lax.axis_index("group")
        tensor = lax.axis_index("tensor")
        self.e, self.h = tensor // 2, lax.rem(tensor, 2)

    def device(self, x=None, e=None, h=None, c=None):
        x = self.x if x is None else x
        e = self.e if e is None else e
        h = self.h if h is None else h
        c = self.c if c is None else c
        return (x, 2 * e + h, c)

    def step_x(self, d):
        return lax.rem(self.x + (d + self.n_dp), self.n_dp)

    def step_e(self, d):
        return lax.rem(self.e + (d + self.experts), self.experts)

    def cols_c(self, c):
        return pl.ds(pl.multiple_of(c * self.half, self.half), self.half)

    def cols_h(self, h, c):
        return pl.ds(pl.multiple_of(c * self.half + h * self.quarter, self.quarter), self.quarter)

    def cols_e(self, e, h, c):
        start = c * self.half + h * self.quarter + e * self.piece
        return pl.ds(pl.multiple_of(start, self.piece), self.piece)


class Sender:
    def __init__(self, send_sems, recv_sems):
        self.send_sems, self.recv_sems, self.copies = send_sems, recv_sems, []

    def start(self, src, dst, device):
        k = len(self.copies)
        copy = pltpu.make_async_remote_copy(
            src_ref=src,
            dst_ref=dst,
            send_sem=self.send_sems.at[k],
            recv_sem=self.recv_sems.at[k],
            device_id=device,
            device_id_type=MESH,
        )
        copy.start()
        self.copies.append(copy)
        return copy

    def finish(self):
        for copy in self.copies:
            copy.wait_send()


def greet(devices):
    barrier = pltpu.get_barrier_semaphore()
    for device in devices:
        pl.semaphore_signal(barrier, inc=1, device_id=device, device_id_type=MESH)
    pl.semaphore_wait(barrier, len(devices))


def forward(place, sender, ref, where, **to):
    return sender.start(ref.at[where], ref.at[where], place.device(**to))


def gather_start(place, sender, out):
    here = place
    where = (slice(None), here.cols_e(here.e, here.h, here.c))
    return [None] + [
        forward(here, sender, out, where, e=here.step_e(d)) for d in range(1, here.experts)
    ]


def gather_pass(place, sender, out, over_e):
    here = place
    over_h, over_c = [], []
    for d in range(here.experts):
        where = (slice(None), here.cols_e(here.step_e(-d), here.h, here.c))
        if d:
            over_e[d].wait_recv()
        over_h.append(forward(here, sender, out, where, h=1 - here.h))
        over_c.append(forward(here, sender, out, where, c=1 - here.c))
    return over_h, over_c


def gather_halves(place, sender, out, over_h, over_c):
    here = place
    for d in range(here.experts):
        where = (slice(None), here.cols_e(here.step_e(-d), 1 - here.h, here.c))
        over_h[d].wait_recv()
        over_c.append(forward(here, sender, out, where, c=1 - here.c))


def gather_and_dispatch(place, sender, over_e, hidden, select_t, rows, rows_of, work):
    here = place
    steps_x = range(1, here.n_dp)

    def pick(cols):
        rows[rows_of(here.x), cols] = jnp.dot(
            select_t[...], hidden[:, cols], preferred_element_type=F32
        ).astype(BF16)

    over_h, over_c, over_x, rows_h, rows_c = {}, [], {}, {}, []
    for d in range(here.experts):
        cols = here.cols_e(here.step_e(-d), here.h, here.c)
        if d:
            over_e[d].wait_recv()
        over_h[d] = forward(here, sender, hidden, (slice(None), cols), h=1 - here.h)
        over_c.append(forward(here, sender, hidden, (slice(None), cols), c=1 - here.c))
        pick(cols)
        for s in steps_x:
            over_x[d, s] = forward(
                here, sender, rows, (rows_of(here.x), cols), x=here.step_x(s)
            )
    for d in range(here.experts):
        cols = here.cols_e(here.step_e(-d), here.h, here.c)
        for s in steps_x:
            over_x[d, s].wait_recv()
            where = (rows_of(here.step_x(-s)), cols)
            rows_h[d, s] = forward(here, sender, rows, where, h=1 - here.h)
            rows_c.append(forward(here, sender, rows, where, c=1 - here.c))
        other = here.cols_e(here.step_e(-d), 1 - here.h, here.c)
        over_h[d].wait_recv()
        over_c.append(forward(here, sender, hidden, (slice(None), other), c=1 - here.c))
        pick(other)
    work(here.cols_h(here.h, here.c))
    for d in range(here.experts):
        cols = here.cols_e(here.step_e(-d), 1 - here.h, here.c)
        for s in steps_x:
            rows_h[d, s].wait_recv()
            where = (rows_of(here.step_x(-s)), cols)
            rows_c.append(forward(here, sender, rows, where, c=1 - here.c))
    for copy in over_c:
        copy.wait_recv()
    pick(here.cols_c(1 - here.c))
    early = here.experts * (here.n_dp - 1)
    for copy in rows_c[:early]:
        copy.wait_recv()
    work(here.cols_h(here.h, 1 - here.c))
    work(here.cols_h(1 - here.h, here.c))
    for copy in rows_c[early:]:
        copy.wait_recv()
    work(here.cols_h(1 - here.h, 1 - here.c))


def tiles(extent, most):
    size = 128
    while size * 2 <= most and extent % (size * 2) == 0:
        size *= 2
    return size, extent // size


def layer_kernel(
    n_dp,
    experts,
    mixer_ref,
    routes_t,
    cotangent_ref,
    resid_ref,
    gain_ref,
    router_ref,
    gate_hbm,
    up_hbm,
    down_hbm,
    proj_hbm,
    layer_ref,
    mixer_cot_ref,
    act_ref,
    out_cot_ref,
    w_gate,
    w_up,
    w_down,
    w_proj,
    own,
    hidden,
    mix,
    cot,
    select,
    select_t,
    slot_cot,
    rows,
    own_out,
    own_in,
    swap_in,
    swapped,
    half_in,
    half_sum,
    hidden_parts,
    pair_in,
    paired,
    parts,
    tokens,
    pieces,
    d_gate,
    d_up,
    raw_cot,
    pre_gate,
    pre_up,
    gates,
    slopes,
    squares,
    logits,
    weighted,
    inv_rows,
    inner,
    cot_proj,
    hidden_proj,
    change_proj,
    load_sems,
    send_sems,
    recv_sems,
):
    row_count, width = resid_ref.shape
    slots = slot_cot.shape[0]
    capacity = slots // n_dp
    here = Place(n_dp, experts, width)
    sender = Sender(send_sems, recv_sems)

    def rows_of(x):
        return pl.ds(pl.multiple_of(x * capacity, capacity), capacity)

    loads = [
        pltpu.make_async_copy(src, dst, load_sems.at[k])
        for k, (src, dst) in enumerate(((down_hbm, w_down), (gate_hbm, w_gate), (up_hbm, w_up)))
    ]
    blocks = [(flip, other) for other in (1, 0) for flip in (1, 0)]
    proj_loads = []
    for k, (flip, other) in enumerate(blocks):
        cols = here.cols_h(lax.rem(here.h + flip, 2), lax.rem(here.c + other, 2))
        load = pltpu.make_async_copy(
            proj_hbm.at[:, cols], w_proj.at[:, cols], load_sems.at[3 + k]
        )
        load.start()
        proj_loads.append((cols, load))

    plane = [(d, flip) for flip in (1, 0) for d in range(n_dp)]
    devices = [here.device(c=1 - here.c)]
    devices += [here.device(e=here.step_e(d)) for d in range(1, experts)]
    devices += [
        here.device(x=here.step_x(d), h=lax.rem(here.h + flip, 2)) for d, flip in plane if d or flip
    ]
    greet(devices)

    hit_t = ((routes_t[0:1, :] == here.e) | (routes_t[1:2, :] == here.e)).astype(F32)
    row = lax.broadcasted_iota(jnp.int32, (row_count, row_count), 0)
    col = lax.broadcasted_iota(jnp.int32, (row_count, row_count), 1)
    hit = jnp.sum(jnp.where(row == col, hit_t, 0.0), axis=1, keepdims=True)
    slot = jnp.sum(jnp.where(col < row, hit_t, 0.0), axis=1, keepdims=True)
    slot_t = jnp.sum(jnp.where(row < col, hit, 0.0), axis=0, keepdims=True)
    number = lax.broadcasted_iota(jnp.int32, (row_count, capacity), 1).astype(F32)
    number_t = lax.broadcasted_iota(jnp.int32, (capacity, row_count), 0).astype(F32)
    select[...] = jnp.where(slot == number, hit, 0.0).astype(BF16)
    select_t[...] = jnp.where(slot_t == number_t, hit_t, 0.0).astype(BF16)

    half_cols = here.cols_c(here.c)
    own_rows = rows_of(here.x)

    def pick_cot(cols):
        slot_cot[own_rows, cols] = jnp.dot(
            select_t[...], cotangent_ref[:, cols], preferred_element_type=F32
        ).astype(BF16)

    pick_cot(half_cols)
    replicas = [
        forward(here, sender, slot_cot, (own_rows, half_cols), x=here.step_x(d))
        for d in range(1, n_dp)
    ]

    swaps = []
    for (flip, other), (cols, load) in zip(blocks, proj_loads):
        load.wait()
        own[:, cols] = jnp.dot(
            mixer_ref[...], w_proj[:, cols], preferred_element_type=F32
        ).astype(BF16)
        if other:
            there = here.cols_h(lax.rem(here.h + flip, 2), 0)
            swaps.append(
                sender.start(own.at[:, cols], swap_in.at[:, there], here.device(c=1 - here.c))
            )
    for load in loads:
        load.start()
    order = list(range(1, experts)) + [0]
    halves = {}
    for flip in (1, 0):
        h = lax.rem(here.h + flip, 2)
        there = here.cols_h(h, 0)
        swaps[1 - flip].wait_recv()
        swapped[:, there] = (
            own[:, here.cols_h(h, here.c)].astype(F32) + swap_in[:, there].astype(F32)
        ).astype(BF16)
        if flip:
            for d in order:
                halves[d] = sender.start(
                    swapped.at[:, here.cols_e(here.step_e(d), h, 0)],
                    half_in.at[d],
                    here.device(h=h),
                )
    pick_cot(here.cols_c(1 - here.c))
    arrivals = {}
    for d in order:
        halves[d].wait_recv()
        total = swapped[:, here.cols_e(here.step_e(d), here.h, 0)].astype(F32)
        total = total + half_in[d].astype(F32)
        if d:
            half_sum[d - 1] = total.astype(BF16)
            arrivals[d] = sender.start(
                half_sum.at[d - 1], hidden_parts.at[d - 1], here.device(e=here.step_e(d))
            )
    shared = []
    for d in range(1, n_dp):
        replicas[d - 1].wait_recv()
        where = (rows_of(here.step_x(-d)), half_cols)
        shared.append(forward(here, sender, slot_cot, where, c=1 - here.c))
    own_cols = here.cols_e(here.e, here.h, here.c)
    total = total + resid_ref[:, own_cols].astype(F32)
    for d in range(1, experts):
        arrivals[d].wait_recv()
        total = total + hidden_parts[d - 1].astype(F32)
    hidden[:, own_cols] = total.astype(BF16)
    over_e = gather_start(here, sender, hidden)

    for copy in shared:
        copy.wait_recv()
    loads[0].wait()
    depth, steps = tiles(width, 1024)
    raw_cot[...] = jnp.zeros_like(raw_cot)

    @pl.loop(0, steps)
    def _(k):
        cols = pl.ds(pl.multiple_of(k * depth, depth), depth)
        raw_cot[...] += contract_cols(slot_cot[:, cols], w_down[:, cols])

    router_row = router_ref.at[pl.ds(here.e, 1), :]

    for ref in (pre_gate, pre_up, squares, logits):
        ref[...] = jnp.zeros_like(ref)
    loads[1].wait()
    loads[2].wait()

    def expert_columns(cols):
        @pl.loop(0, slots // 16)
        def _(k):
            block = pl.ds(pl.multiple_of(k * 16, 16), 16)
            value = rows[block, cols].astype(F32)
            scaled = (value * gain_ref[:, cols]).astype(BF16)
            own_in[block, cols] = scaled
            squares[block, :] += jnp.sum(value * value, axis=1, keepdims=True)
            logits[block, :] += jnp.sum(
                scaled.astype(F32) * router_row[:, cols], axis=1, keepdims=True
            )

        pre_gate[...] += jnp.dot(own_in[:, cols], w_gate[cols, :], preferred_element_type=F32)
        pre_up[...] += jnp.dot(own_in[:, cols], w_up[cols, :], preferred_element_type=F32)

    gather_and_dispatch(
        here, sender, over_e, hidden, select_t, rows, rows_of, expert_columns
    )
    squares[...] = lax.rsqrt(squares[...] / width + 1e-05)
    gates[...] = jax.nn.sigmoid(logits[...] * squares[...])

    @pl.loop(0, slots // 16)
    def _(k):
        block = pl.ds(pl.multiple_of(k * 16, 16), 16)
        gate, raw, inv_rms = gates[block, :], raw_cot[block, :], squares[block, :]
        z, up = pre_gate[block, :] * inv_rms, pre_up[block, :] * inv_rms
        sig = jax.nn.sigmoid(z)
        act = (z * sig * up).astype(BF16)
        act_ref[block, :] = act
        act_cot = gate * raw
        d_gate[block, :] = (act_cot * up * sig * (1.0 + z * (1.0 - sig))).astype(BF16)
        d_up[block, :] = (act_cot * z * sig).astype(BF16)
        gate_cot = jnp.sum(act.astype(F32) * raw, axis=1, keepdims=True)
        slopes[block, :] = gate_cot * gate * (1.0 - gate)

    span, spans = tiles(here.quarter, 512)

    def forward_tile(cols):
        own_out[:, cols] = (
            gates[...] * jnp.dot(act_ref[...], w_down[:, cols], preferred_element_type=F32)
        ).astype(BF16)

    def backward_tile(cols):
        own_in[:, cols] = (
            contract_cols(d_gate[...], w_gate[cols, :])
            + contract_cols(d_up[...], w_up[cols, :])
            + slopes[...] * router_row[:, cols]
        ).astype(BF16)

    crossing = {}
    for i, (source, tile) in enumerate(((own_out, forward_tile), (own_in, backward_tile))):

        def fill(h, c, tile=tile):
            first = c * here.half + h * here.quarter

            @pl.loop(0, spans)
            def _(k):
                tile(pl.ds(pl.multiple_of(first + k * span, span), span))

        swaps = {}
        for flip in (1, 0):
            h = lax.rem(here.h + flip, 2)
            fill(h, 1 - here.c)
            for k, (d, f) in enumerate(plane):
                if f == flip:
                    swaps[k] = sender.start(
                        source.at[rows_of(here.step_x(d)), here.cols_h(h, 1 - here.c)],
                        pair_in.at[i, k],
                        here.device(c=1 - here.c),
                    )
        for flip in (1, 0):
            h = lax.rem(here.h + flip, 2)
            fill(h, here.c)
            for k, (d, f) in enumerate(plane):
                if f == flip:
                    swaps[k].wait_recv()
                    paired[i, k] = (
                        source[rows_of(here.step_x(d)), here.cols_h(h, here.c)].astype(F32)
                        + pair_in[i, k].astype(F32)
                    ).astype(BF16)
                    if d or f:
                        crossing[i, k] = sender.start(
                            paired.at[i, k], parts.at[i, k], here.device(x=here.step_x(d), h=h)
                        )

    @pl.loop(0, slots // 16)
    def _(k):
        block = pl.ds(pl.multiple_of(k * 16, 16), 16)
        out_cot_ref[block, :] = (gates[block, :] * slot_cot[block, :].astype(F32)).astype(BF16)

    @pl.loop(0, row_count // 16)
    def _(k):
        block = pl.ds(pl.multiple_of(k * 16, 16), 16)
        value = hidden[block, :].astype(F32)
        inv_rows[block, :] = lax.rsqrt(jnp.mean(value * value, axis=1, keepdims=True) + 1e-05)

    cot_proj[...] = contract_cols(cotangent_ref[...], w_proj[...])
    hidden_proj[...] = contract_cols(hidden[...], w_proj[...])
    inner[...] = jnp.zeros_like(inner)
    change_proj[...] = jnp.zeros_like(change_proj)

    own_slot = plane.index((0, 0))
    mine_cols = pl.ds(pl.multiple_of(here.e * here.piece, here.piece), here.piece)
    started = []
    for i, result in enumerate((mix, cot)):
        total = paired[i, own_slot].astype(F32)
        for k in range(len(plane)):
            if k != own_slot:
                crossing[i, k].wait_recv()
                total = total + parts[i, k].astype(F32)
        tokens[i] = jnp.dot(select[...], total.astype(BF16), preferred_element_type=F32).astype(
            BF16
        )
        scattered = []
        for d in range(1, experts):
            e = here.step_e(d)
            cols = pl.ds(pl.multiple_of(e * here.piece, here.piece), here.piece)
            scattered.append(
                sender.start(tokens.at[i, :, cols], pieces.at[i, d - 1], here.device(e=e))
            )
        if i:
            mix_passed = gather_pass(here, sender, mix, started[0])
        total = tokens[i, :, mine_cols].astype(F32)
        for d in range(1, experts):
            scattered[d - 1].wait_recv()
            total = total + pieces[i, d - 1].astype(F32)
        result[:, own_cols] = total.astype(BF16)
        started.append(gather_start(here, sender, result))
    cot_passed = gather_pass(here, sender, cot, started[1])
    gather_halves(here, sender, mix, *mix_passed)
    for copy in mix_passed[1]:
        copy.wait_recv()

    @pl.loop(0, row_count // 16)
    def _(k):
        block = pl.ds(pl.multiple_of(k * 16, 16), 16)
        layer_ref[block, :] = (hidden[block, :].astype(F32) + mix[block, :].astype(F32)).astype(
            BF16
        )

    def change_columns(cols):
        @pl.loop(0, row_count // 16)
        def _(k):
            block = pl.ds(pl.multiple_of(k * 16, 16), 16)
            scaled = cot[block, cols].astype(F32) * gain_ref[:, cols]
            weighted[block, cols] = scaled.astype(BF16)
            inner[block, :] += jnp.sum(
                scaled * hidden[block, cols].astype(F32), axis=1, keepdims=True
            )

        change_proj[...] += contract_cols(weighted[:, cols], w_proj[:, cols])

    gather_halves(here, sender, cot, *cot_passed)
    change_columns(here.cols_h(here.h, here.c))
    from_core = cot_passed[1]
    for copy in from_core[:experts]:
        copy.wait_recv()
    change_columns(here.cols_h(here.h, 1 - here.c))
    change_columns(here.cols_h(1 - here.h, here.c))
    for copy in from_core[experts:]:
        copy.wait_recv()
    change_columns(here.cols_h(1 - here.h, 1 - here.c))
    inv_rms = inv_rows[...]
    along = inv_rms * inv_rms * inv_rms * (inner[...] / width)
    mixer_cot_ref[...] = (
        cot_proj[...] + inv_rms * change_proj[...] - along * hidden_proj[...]
    ).astype(BF16)
    sender.finish()


def result_kernel(act_ref, out_cot_ref, layer_ref, mixer_cot_ref, down_ref, layer_out, mixer_out):
    down_ref[...] = contract_rows(act_ref[...], out_cot_ref[...]).astype(BF16)
    layer_out[...] = layer_ref[...]
    mixer_out[...] = mixer_cot_ref[...]


def on_device(
    n_dp, resid, mixer_out, out_proj, norm_gain, router, routes, w_gate, w_up, w_down, cotangent
):
    row_count, width = resid.shape
    experts = router.shape[1]
    capacity = min(row_count, 3 * row_count // experts)
    half, quarter, piece = width // 2, width // 4, width // (4 * experts)
    slots, units, plane = n_dp * capacity, w_gate.shape[2], 2 * n_dp
    gathers = 4 * experts - 1
    dispatch = 4 * experts * (n_dp - 1)
    reduce = 2 + 2 * (n_dp - 1) + 2 * experts - 1
    combine = 2 * (plane + plane - 1 + experts - 1 + gathers)
    copies = reduce + gathers + dispatch + combine
    whole = pl.BlockSpec(memory_space=pltpu.VMEM)
    remote = pl.BlockSpec(memory_space=pl.ANY)
    layer_out, grad_mixer, activated, out_cot = pl.pallas_call(
        functools.partial(layer_kernel, n_dp, experts),
        out_shape=[
            jax.ShapeDtypeStruct((row_count, width), BF16),
            jax.ShapeDtypeStruct(mixer_out.shape, BF16),
            jax.ShapeDtypeStruct((slots, units), BF16),
            jax.ShapeDtypeStruct((slots, width), BF16),
        ],
        in_specs=[whole] * 6 + [remote] * 4,
        out_specs=[whole] * 4,
        scratch_shapes=[
            pltpu.VMEM((width, units), BF16),
            pltpu.VMEM((width, units), BF16),
            pltpu.VMEM((units, width), BF16),
            pltpu.VMEM(out_proj.shape, BF16),
            pltpu.VMEM((row_count, width), BF16),
            pltpu.VMEM((row_count, width), BF16),
            pltpu.VMEM((row_count, width), BF16),
            pltpu.VMEM((row_count, width), BF16),
            pltpu.VMEM((row_count, capacity), BF16),
            pltpu.VMEM((capacity, row_count), BF16),
            pltpu.VMEM((slots, width), BF16),
            pltpu.VMEM((slots, width), BF16),
            pltpu.VMEM((slots, width), BF16),
            pltpu.VMEM((slots, width), BF16),
            pltpu.VMEM((row_count, half), BF16),
            pltpu.VMEM((row_count, half), BF16),
            pltpu.VMEM((experts, row_count, piece), BF16),
            pltpu.VMEM((experts - 1, row_count, piece), BF16),
            pltpu.VMEM((experts - 1, row_count, piece), BF16),
            pltpu.VMEM((2, plane, capacity, quarter), BF16),
            pltpu.VMEM((2, plane, capacity, quarter), BF16),
            pltpu.VMEM((2, plane, capacity, quarter), BF16),
            pltpu.VMEM((2, row_count, quarter), BF16),
            pltpu.VMEM((2, experts - 1, row_count, piece), BF16),
            pltpu.VMEM((slots, units), BF16),
            pltpu.VMEM((slots, units), BF16),
            pltpu.VMEM((slots, units), F32),
            pltpu.VMEM((slots, units), F32),
            pltpu.VMEM((slots, units), F32),
            pltpu.VMEM((slots, 1), F32),
            pltpu.VMEM((slots, 1), F32),
            pltpu.VMEM((slots, 1), F32),
            pltpu.VMEM((slots, 1), F32),
            pltpu.VMEM((row_count, width), BF16),
            pltpu.VMEM((row_count, 1), F32),
            pltpu.VMEM((row_count, 1), F32),
            pltpu.VMEM(mixer_out.shape, F32),
            pltpu.VMEM(mixer_out.shape, F32),
            pltpu.VMEM(mixer_out.shape, F32),
            pltpu.SemaphoreType.DMA((7,)),
            pltpu.SemaphoreType.DMA((copies,)),
            pltpu.SemaphoreType.DMA((copies,)),
        ],
        compiler_params=pltpu.CompilerParams(
            collective_id=0, has_side_effects=True, vmem_limit_bytes=VMEM_MIB * 1024 * 1024
        ),
    )(
        mixer_out,
        routes.T,
        cotangent,
        resid,
        norm_gain[None],
        router.T,
        w_gate[0],
        w_up[0],
        w_down[0],
        out_proj,
    )
    span, spans = tiles(width, 1024)
    grad_down, layer_out, grad_mixer = pl.pallas_call(
        result_kernel,
        grid=(spans,),
        out_shape=[
            jax.ShapeDtypeStruct((units, width), BF16),
            jax.ShapeDtypeStruct((row_count, width), BF16),
            jax.ShapeDtypeStruct(mixer_out.shape, BF16),
        ],
        in_specs=[
            pl.BlockSpec((slots, units), lambda j: (0, 0)),
            pl.BlockSpec((slots, span), lambda j: (0, j)),
            pl.BlockSpec((row_count, span), lambda j: (0, j)),
            pl.BlockSpec(mixer_out.shape, lambda j: (0, 0)),
        ],
        out_specs=[
            pl.BlockSpec((units, span), lambda j: (0, j)),
            pl.BlockSpec((row_count, span), lambda j: (0, j)),
            pl.BlockSpec(mixer_out.shape, lambda j: (0, 0)),
        ],
        compiler_params=pltpu.CompilerParams(vmem_limit_bytes=32 * 1024 * 1024),
    )(activated, out_cot, layer_out, grad_mixer)
    grad_down = grad_down[None]
    return (layer_out, grad_mixer, grad_down)


def solution(mesh):
    placed = (
        P("dp", None),
        P("dp", ("tensor", "group")),
        P(("tensor", "group"), None),
        P(),
        P(),
        P("dp", None),
        P("tensor", None, ("dp", "group")),
        P("tensor", None, ("dp", "group")),
        P("tensor", ("dp", "group"), None),
        P("dp", None),
    )
    return jax.shard_map(
        functools.partial(on_device, mesh.shape["dp"]),
        mesh=mesh,
        in_specs=placed,
        out_specs=(P("dp", None), P("dp", ("tensor", "group")), P("tensor", ("dp", "group"), None)),
        check_vma=False,
    )
```

```python
import functools

import jax
import jax.numpy as jnp
from jax import lax
from jax.experimental import pallas as pl
from jax.experimental.pallas import tpu as pltpu
from jax.sharding import PartitionSpec as P

MESH = pl.DeviceIdType.MESH
F32 = jnp.float32
BF16 = jnp.bfloat16
VMEM_MIB = 60


def contract_rows(left, right):
    return lax.dot_general(left, right, (((0,), (0,)), ((), ())), preferred_element_type=F32)


def contract_cols(left, right):
    return lax.dot_general(left, right, (((1,), (1,)), ((), ())), preferred_element_type=F32)


class Place:
    def __init__(self, n_dp, experts, width):
        self.n_dp, self.experts = n_dp, experts
        self.half, self.quarter, self.piece = width // 2, width // 4, width // (4 * experts)
        self.x, self.c = lax.axis_index("dp"), lax.axis_index("group")
        tensor = lax.axis_index("tensor")
        self.e, self.h = tensor // 2, lax.rem(tensor, 2)

    def device(self, x=None, e=None, h=None, c=None):
        x = self.x if x is None else x
        e = self.e if e is None else e
        h = self.h if h is None else h
        c = self.c if c is None else c
        return (x, 2 * e + h, c)

    def step_x(self, d):
        return lax.rem(self.x + (d + self.n_dp), self.n_dp)

    def step_e(self, d):
        return lax.rem(self.e + (d + self.experts), self.experts)

    def cols_c(self, c):
        return pl.ds(pl.multiple_of(c * self.half, self.half), self.half)

    def cols_h(self, h, c):
        return pl.ds(pl.multiple_of(c * self.half + h * self.quarter, self.quarter), self.quarter)

    def cols_e(self, e, h, c):
        start = c * self.half + h * self.quarter + e * self.piece
        return pl.ds(pl.multiple_of(start, self.piece), self.piece)


class Sender:
    def __init__(self, send_sems, recv_sems):
        self.send_sems, self.recv_sems, self.copies = send_sems, recv_sems, []

    def start(self, src, dst, device):
        k = len(self.copies)
        copy = pltpu.make_async_remote_copy(
            src_ref=src,
            dst_ref=dst,
            send_sem=self.send_sems.at[k],
            recv_sem=self.recv_sems.at[k],
            device_id=device,
            device_id_type=MESH,
        )
        copy.start()
        self.copies.append(copy)
        return copy

    def finish(self):
        for copy in self.copies:
            copy.wait_send()


def greet(devices):
    barrier = pltpu.get_barrier_semaphore()
    for device in devices:
        pl.semaphore_signal(barrier, inc=1, device_id=device, device_id_type=MESH)
    pl.semaphore_wait(barrier, len(devices))


def forward(place, sender, ref, where, **to):
    return sender.start(ref.at[where], ref.at[where], place.device(**to))


def gather_start(place, sender, out):
    here = place
    where = (slice(None), here.cols_e(here.e, here.h, here.c))
    return [None] + [
        forward(here, sender, out, where, e=here.step_e(d)) for d in range(1, here.experts)
    ]


def gather_pass(place, sender, out, over_e):
    here = place
    over_h, over_c = [], []
    for d in range(here.experts):
        where = (slice(None), here.cols_e(here.step_e(-d), here.h, here.c))
        if d:
            over_e[d].wait_recv()
        over_h.append(forward(here, sender, out, where, h=1 - here.h))
        over_c.append(forward(here, sender, out, where, c=1 - here.c))
    return over_h, over_c


def gather_finish(place, sender, out, over_h, over_c):
    here = place
    for d in range(here.experts):
        where = (slice(None), here.cols_e(here.step_e(-d), 1 - here.h, here.c))
        over_h[d].wait_recv()
        over_c.append(forward(here, sender, out, where, c=1 - here.c))
    for copy in over_c:
        copy.wait_recv()


def gather_and_dispatch(place, sender, over_e, hidden, select_t, rows, rows_of):
    here = place
    steps_x = range(1, here.n_dp)

    def pick(cols):
        rows[rows_of(here.x), cols] = jnp.dot(
            select_t[...], hidden[:, cols], preferred_element_type=F32
        ).astype(BF16)

    over_h, over_c, over_x, rows_h, rows_c = {}, [], {}, {}, []
    for d in range(here.experts):
        cols = here.cols_e(here.step_e(-d), here.h, here.c)
        if d:
            over_e[d].wait_recv()
        over_h[d] = forward(here, sender, hidden, (slice(None), cols), h=1 - here.h)
        over_c.append(forward(here, sender, hidden, (slice(None), cols), c=1 - here.c))
        pick(cols)
        for s in steps_x:
            over_x[d, s] = forward(
                here, sender, rows, (rows_of(here.x), cols), x=here.step_x(s)
            )
    for d in range(here.experts):
        cols = here.cols_e(here.step_e(-d), here.h, here.c)
        for s in steps_x:
            over_x[d, s].wait_recv()
            where = (rows_of(here.step_x(-s)), cols)
            rows_h[d, s] = forward(here, sender, rows, where, h=1 - here.h)
            rows_c.append(forward(here, sender, rows, where, c=1 - here.c))
        other = here.cols_e(here.step_e(-d), 1 - here.h, here.c)
        over_h[d].wait_recv()
        over_c.append(forward(here, sender, hidden, (slice(None), other), c=1 - here.c))
        pick(other)
    for d in range(here.experts):
        cols = here.cols_e(here.step_e(-d), 1 - here.h, here.c)
        for s in steps_x:
            rows_h[d, s].wait_recv()
            where = (rows_of(here.step_x(-s)), cols)
            rows_c.append(forward(here, sender, rows, where, c=1 - here.c))
    for copy in over_c:
        copy.wait_recv()
    pick(here.cols_c(1 - here.c))
    return rows_c


def tiles(extent, most):
    size = 128
    while size * 2 <= most and extent % (size * 2) == 0:
        size *= 2
    return size, extent // size


def layer_kernel(
    n_dp,
    experts,
    mixer_ref,
    routes_t,
    cotangent_ref,
    resid_ref,
    gain_ref,
    router_ref,
    gate_hbm,
    up_hbm,
    down_hbm,
    proj_hbm,
    layer_ref,
    mixer_cot_ref,
    act_ref,
    out_cot_ref,
    w_gate,
    w_up,
    w_down,
    w_proj,
    own,
    hidden,
    mix,
    cot,
    select,
    select_t,
    slot_cot,
    rows,
    own_out,
    own_in,
    swap_in,
    swapped,
    half_in,
    half_sum,
    hidden_parts,
    pair_in,
    paired,
    parts,
    tokens,
    pieces,
    d_gate,
    d_up,
    raw_cot,
    pre_gate,
    pre_up,
    gates,
    slopes,
    hidden_cot,
    inv_rows,
    load_sems,
    send_sems,
    recv_sems,
):
    row_count, width = resid_ref.shape
    slots = slot_cot.shape[0]
    capacity = slots // n_dp
    here = Place(n_dp, experts, width)
    sender = Sender(send_sems, recv_sems)

    def rows_of(x):
        return pl.ds(pl.multiple_of(x * capacity, capacity), capacity)

    loads = [
        pltpu.make_async_copy(src, dst, load_sems.at[k])
        for k, (src, dst) in enumerate(((down_hbm, w_down), (gate_hbm, w_gate), (up_hbm, w_up)))
    ]
    blocks = [(flip, other) for other in (1, 0) for flip in (1, 0)]
    proj_loads = []
    for k, (flip, other) in enumerate(blocks):
        cols = here.cols_h(lax.rem(here.h + flip, 2), lax.rem(here.c + other, 2))
        load = pltpu.make_async_copy(
            proj_hbm.at[:, cols], w_proj.at[:, cols], load_sems.at[3 + k]
        )
        load.start()
        proj_loads.append((cols, load))

    plane = [(d, flip) for flip in (1, 0) for d in range(n_dp)]
    devices = [here.device(c=1 - here.c)]
    devices += [here.device(e=here.step_e(d)) for d in range(1, experts)]
    devices += [
        here.device(x=here.step_x(d), h=lax.rem(here.h + flip, 2)) for d, flip in plane if d or flip
    ]
    greet(devices)

    hit_t = ((routes_t[0:1, :] == here.e) | (routes_t[1:2, :] == here.e)).astype(F32)
    row = lax.broadcasted_iota(jnp.int32, (row_count, row_count), 0)
    col = lax.broadcasted_iota(jnp.int32, (row_count, row_count), 1)
    hit = jnp.sum(jnp.where(row == col, hit_t, 0.0), axis=1, keepdims=True)
    slot = jnp.sum(jnp.where(col < row, hit_t, 0.0), axis=1, keepdims=True)
    slot_t = jnp.sum(jnp.where(row < col, hit, 0.0), axis=0, keepdims=True)
    number = lax.broadcasted_iota(jnp.int32, (row_count, capacity), 1).astype(F32)
    number_t = lax.broadcasted_iota(jnp.int32, (capacity, row_count), 0).astype(F32)
    select[...] = jnp.where(slot == number, hit, 0.0).astype(BF16)
    select_t[...] = jnp.where(slot_t == number_t, hit_t, 0.0).astype(BF16)

    half_cols = here.cols_c(here.c)
    own_rows = rows_of(here.x)

    def pick_cot(cols):
        slot_cot[own_rows, cols] = jnp.dot(
            select_t[...], cotangent_ref[:, cols], preferred_element_type=F32
        ).astype(BF16)

    pick_cot(half_cols)
    replicas = [
        forward(here, sender, slot_cot, (own_rows, half_cols), x=here.step_x(d))
        for d in range(1, n_dp)
    ]

    swaps = []
    for (flip, other), (cols, load) in zip(blocks, proj_loads):
        load.wait()
        own[:, cols] = jnp.dot(
            mixer_ref[...], w_proj[:, cols], preferred_element_type=F32
        ).astype(BF16)
        if other:
            there = here.cols_h(lax.rem(here.h + flip, 2), 0)
            swaps.append(
                sender.start(own.at[:, cols], swap_in.at[:, there], here.device(c=1 - here.c))
            )
    for load in loads:
        load.start()
    order = list(range(1, experts)) + [0]
    halves = {}
    for flip in (1, 0):
        h = lax.rem(here.h + flip, 2)
        there = here.cols_h(h, 0)
        swaps[1 - flip].wait_recv()
        swapped[:, there] = (
            own[:, here.cols_h(h, here.c)].astype(F32) + swap_in[:, there].astype(F32)
        ).astype(BF16)
        if flip:
            for d in order:
                halves[d] = sender.start(
                    swapped.at[:, here.cols_e(here.step_e(d), h, 0)],
                    half_in.at[d],
                    here.device(h=h),
                )
    pick_cot(here.cols_c(1 - here.c))
    arrivals = {}
    for d in order:
        halves[d].wait_recv()
        total = swapped[:, here.cols_e(here.step_e(d), here.h, 0)].astype(F32)
        total = total + half_in[d].astype(F32)
        if d:
            half_sum[d - 1] = total.astype(BF16)
            arrivals[d] = sender.start(
                half_sum.at[d - 1], hidden_parts.at[d - 1], here.device(e=here.step_e(d))
            )
    shared = []
    for d in range(1, n_dp):
        replicas[d - 1].wait_recv()
        where = (rows_of(here.step_x(-d)), half_cols)
        shared.append(forward(here, sender, slot_cot, where, c=1 - here.c))
    own_cols = here.cols_e(here.e, here.h, here.c)
    total = total + resid_ref[:, own_cols].astype(F32)
    for d in range(1, experts):
        arrivals[d].wait_recv()
        total = total + hidden_parts[d - 1].astype(F32)
    hidden[:, own_cols] = total.astype(BF16)
    over_e = gather_start(here, sender, hidden)

    for copy in shared:
        copy.wait_recv()
    loads[0].wait()
    depth, steps = tiles(width, 1024)
    raw_cot[...] = jnp.zeros_like(raw_cot)

    @pl.loop(0, steps)
    def _(k):
        cols = pl.ds(pl.multiple_of(k * depth, depth), depth)
        raw_cot[...] += contract_cols(slot_cot[:, cols], w_down[:, cols])

    router_row = router_ref.at[pl.ds(here.e, 1), :]
    rows_c = gather_and_dispatch(here, sender, over_e, hidden, select_t, rows, rows_of)

    def norm_rows(x):
        @pl.loop(0, capacity // 16)
        def _(k):
            block = pl.ds(pl.multiple_of(x * capacity + k * 16, 16), 16)
            value = rows[block, :].astype(F32)
            inv_rms = lax.rsqrt(jnp.mean(value * value, axis=1, keepdims=True) + 1e-05)
            normed = (value * inv_rms * gain_ref[...]).astype(BF16)
            own_in[block, :] = normed
            logit = jnp.sum(normed.astype(F32) * router_row[...], axis=1, keepdims=True)
            gate = jax.nn.sigmoid(logit)
            gates[block, :] = gate

    norm_rows(here.x)
    for copy in rows_c:
        copy.wait_recv()
    for d in range(1, n_dp):
        norm_rows(here.step_x(d))

    loads[1].wait()
    loads[2].wait()
    pre_gate[...] = jnp.zeros_like(pre_gate)
    pre_up[...] = jnp.zeros_like(pre_up)

    @pl.loop(0, steps)
    def _(k):
        cols = pl.ds(pl.multiple_of(k * depth, depth), depth)
        pre_gate[...] += jnp.dot(own_in[:, cols], w_gate[cols, :], preferred_element_type=F32)
        pre_up[...] += jnp.dot(own_in[:, cols], w_up[cols, :], preferred_element_type=F32)

    @pl.loop(0, slots // 16)
    def _(k):
        block = pl.ds(pl.multiple_of(k * 16, 16), 16)
        gate, raw = gates[block, :], raw_cot[block, :]
        z, up = pre_gate[block, :], pre_up[block, :]
        sig = jax.nn.sigmoid(z)
        act = (z * sig * up).astype(BF16)
        act_ref[block, :] = act
        act_cot = gate * raw
        d_gate[block, :] = (act_cot * up * sig * (1.0 + z * (1.0 - sig))).astype(BF16)
        d_up[block, :] = (act_cot * z * sig).astype(BF16)
        gate_cot = jnp.sum(act.astype(F32) * raw, axis=1, keepdims=True)
        slopes[block, :] = gate_cot * gate * (1.0 - gate)

    span, spans = tiles(here.quarter, 512)

    def forward_tile(cols):
        own_out[:, cols] = (
            gates[...] * jnp.dot(act_ref[...], w_down[:, cols], preferred_element_type=F32)
        ).astype(BF16)

    def backward_tile(cols):
        own_in[:, cols] = (
            contract_cols(d_gate[...], w_gate[cols, :])
            + contract_cols(d_up[...], w_up[cols, :])
            + slopes[...] * router_row[:, cols]
        ).astype(BF16)

    crossing = {}
    for i, (source, tile) in enumerate(((own_out, forward_tile), (own_in, backward_tile))):

        def fill(h, c, tile=tile):
            first = c * here.half + h * here.quarter

            @pl.loop(0, spans)
            def _(k):
                tile(pl.ds(pl.multiple_of(first + k * span, span), span))

        swaps = {}
        for flip in (1, 0):
            h = lax.rem(here.h + flip, 2)
            fill(h, 1 - here.c)
            for k, (d, f) in enumerate(plane):
                if f == flip:
                    swaps[k] = sender.start(
                        source.at[rows_of(here.step_x(d)), here.cols_h(h, 1 - here.c)],
                        pair_in.at[i, k],
                        here.device(c=1 - here.c),
                    )
        for flip in (1, 0):
            h = lax.rem(here.h + flip, 2)
            fill(h, here.c)
            for k, (d, f) in enumerate(plane):
                if f == flip:
                    swaps[k].wait_recv()
                    paired[i, k] = (
                        source[rows_of(here.step_x(d)), here.cols_h(h, here.c)].astype(F32)
                        + pair_in[i, k].astype(F32)
                    ).astype(BF16)
                    if d or f:
                        crossing[i, k] = sender.start(
                            paired.at[i, k], parts.at[i, k], here.device(x=here.step_x(d), h=h)
                        )

    @pl.loop(0, slots // 16)
    def _(k):
        block = pl.ds(pl.multiple_of(k * 16, 16), 16)
        out_cot_ref[block, :] = (gates[block, :] * slot_cot[block, :].astype(F32)).astype(BF16)

    @pl.loop(0, row_count // 16)
    def _(k):
        block = pl.ds(pl.multiple_of(k * 16, 16), 16)
        value = hidden[block, :].astype(F32)
        inv_rows[block, :] = lax.rsqrt(jnp.mean(value * value, axis=1, keepdims=True) + 1e-05)

    own_slot = plane.index((0, 0))
    mine_cols = pl.ds(pl.multiple_of(here.e * here.piece, here.piece), here.piece)
    started = []
    for i, result in enumerate((mix, cot)):
        total = paired[i, own_slot].astype(F32)
        for k in range(len(plane)):
            if k != own_slot:
                crossing[i, k].wait_recv()
                total = total + parts[i, k].astype(F32)
        tokens[i] = jnp.dot(select[...], total.astype(BF16), preferred_element_type=F32).astype(
            BF16
        )
        scattered = []
        for d in range(1, experts):
            e = here.step_e(d)
            cols = pl.ds(pl.multiple_of(e * here.piece, here.piece), here.piece)
            scattered.append(
                sender.start(tokens.at[i, :, cols], pieces.at[i, d - 1], here.device(e=e))
            )
        if i:
            mix_passed = gather_pass(here, sender, mix, started[0])
        total = tokens[i, :, mine_cols].astype(F32)
        for d in range(1, experts):
            scattered[d - 1].wait_recv()
            total = total + pieces[i, d - 1].astype(F32)
        result[:, own_cols] = total.astype(BF16)
        started.append(gather_start(here, sender, result))
    cot_passed = gather_pass(here, sender, cot, started[1])
    gather_finish(here, sender, mix, *mix_passed)

    @pl.loop(0, row_count // 16)
    def _(k):
        block = pl.ds(pl.multiple_of(k * 16, 16), 16)
        layer_ref[block, :] = (hidden[block, :].astype(F32) + mix[block, :].astype(F32)).astype(
            BF16
        )

    gather_finish(here, sender, cot, *cot_passed)

    @pl.loop(0, row_count // 16)
    def _(k):
        block = pl.ds(pl.multiple_of(k * 16, 16), 16)
        value = hidden[block, :].astype(F32)
        inv_rms = inv_rows[block, :]
        weighted = cot[block, :].astype(F32) * gain_ref[...]
        inner_mean = jnp.mean(weighted * value, axis=1, keepdims=True)
        change = inv_rms * weighted - inv_rms * inv_rms * inv_rms * value * inner_mean
        hidden_cot[block, :] = (cotangent_ref[block, :].astype(F32) + change).astype(BF16)

    mixer_cot_ref[...] = contract_cols(hidden_cot[...], w_proj[...]).astype(BF16)
    sender.finish()


def result_kernel(act_ref, out_cot_ref, layer_ref, mixer_cot_ref, down_ref, layer_out, mixer_out):
    down_ref[...] = contract_rows(act_ref[...], out_cot_ref[...]).astype(BF16)
    layer_out[...] = layer_ref[...]
    mixer_out[...] = mixer_cot_ref[...]


def on_device(
    n_dp, resid, mixer_out, out_proj, norm_gain, router, routes, w_gate, w_up, w_down, cotangent
):
    row_count, width = resid.shape
    experts = router.shape[1]
    capacity = min(row_count, 3 * row_count // experts)
    half, quarter, piece = width // 2, width // 4, width // (4 * experts)
    slots, units, plane = n_dp * capacity, w_gate.shape[2], 2 * n_dp
    gathers = 4 * experts - 1
    dispatch = 4 * experts * (n_dp - 1)
    reduce = 2 + 2 * (n_dp - 1) + 2 * experts - 1
    combine = 2 * (plane + plane - 1 + experts - 1 + gathers)
    copies = reduce + gathers + dispatch + combine
    whole = pl.BlockSpec(memory_space=pltpu.VMEM)
    remote = pl.BlockSpec(memory_space=pl.ANY)
    layer_out, grad_mixer, activated, out_cot = pl.pallas_call(
        functools.partial(layer_kernel, n_dp, experts),
        out_shape=[
            jax.ShapeDtypeStruct((row_count, width), BF16),
            jax.ShapeDtypeStruct(mixer_out.shape, BF16),
            jax.ShapeDtypeStruct((slots, units), BF16),
            jax.ShapeDtypeStruct((slots, width), BF16),
        ],
        in_specs=[whole] * 6 + [remote] * 4,
        out_specs=[whole] * 4,
        scratch_shapes=[
            pltpu.VMEM((width, units), BF16),
            pltpu.VMEM((width, units), BF16),
            pltpu.VMEM((units, width), BF16),
            pltpu.VMEM(out_proj.shape, BF16),
            pltpu.VMEM((row_count, width), BF16),
            pltpu.VMEM((row_count, width), BF16),
            pltpu.VMEM((row_count, width), BF16),
            pltpu.VMEM((row_count, width), BF16),
            pltpu.VMEM((row_count, capacity), BF16),
            pltpu.VMEM((capacity, row_count), BF16),
            pltpu.VMEM((slots, width), BF16),
            pltpu.VMEM((slots, width), BF16),
            pltpu.VMEM((slots, width), BF16),
            pltpu.VMEM((slots, width), BF16),
            pltpu.VMEM((row_count, half), BF16),
            pltpu.VMEM((row_count, half), BF16),
            pltpu.VMEM((experts, row_count, piece), BF16),
            pltpu.VMEM((experts - 1, row_count, piece), BF16),
            pltpu.VMEM((experts - 1, row_count, piece), BF16),
            pltpu.VMEM((2, plane, capacity, quarter), BF16),
            pltpu.VMEM((2, plane, capacity, quarter), BF16),
            pltpu.VMEM((2, plane, capacity, quarter), BF16),
            pltpu.VMEM((2, row_count, quarter), BF16),
            pltpu.VMEM((2, experts - 1, row_count, piece), BF16),
            pltpu.VMEM((slots, units), BF16),
            pltpu.VMEM((slots, units), BF16),
            pltpu.VMEM((slots, units), F32),
            pltpu.VMEM((slots, units), F32),
            pltpu.VMEM((slots, units), F32),
            pltpu.VMEM((slots, 1), F32),
            pltpu.VMEM((slots, 1), F32),
            pltpu.VMEM((row_count, width), BF16),
            pltpu.VMEM((row_count, 1), F32),
            pltpu.SemaphoreType.DMA((7,)),
            pltpu.SemaphoreType.DMA((copies,)),
            pltpu.SemaphoreType.DMA((copies,)),
        ],
        compiler_params=pltpu.CompilerParams(
            collective_id=0, has_side_effects=True, vmem_limit_bytes=VMEM_MIB * 1024 * 1024
        ),
    )(
        mixer_out,
        routes.T,
        cotangent,
        resid,
        norm_gain[None],
        router.T,
        w_gate[0],
        w_up[0],
        w_down[0],
        out_proj,
    )
    span, spans = tiles(width, 1024)
    grad_down, layer_out, grad_mixer = pl.pallas_call(
        result_kernel,
        grid=(spans,),
        out_shape=[
            jax.ShapeDtypeStruct((units, width), BF16),
            jax.ShapeDtypeStruct((row_count, width), BF16),
            jax.ShapeDtypeStruct(mixer_out.shape, BF16),
        ],
        in_specs=[
            pl.BlockSpec((slots, units), lambda j: (0, 0)),
            pl.BlockSpec((slots, span), lambda j: (0, j)),
            pl.BlockSpec((row_count, span), lambda j: (0, j)),
            pl.BlockSpec(mixer_out.shape, lambda j: (0, 0)),
        ],
        out_specs=[
            pl.BlockSpec((units, span), lambda j: (0, j)),
            pl.BlockSpec((row_count, span), lambda j: (0, j)),
            pl.BlockSpec(mixer_out.shape, lambda j: (0, 0)),
        ],
        compiler_params=pltpu.CompilerParams(vmem_limit_bytes=VMEM_MIB * 1024 * 1024),
    )(activated, out_cot, layer_out, grad_mixer)
    grad_down = grad_down[None]
    return (layer_out, grad_mixer, grad_down)


def solution(mesh):
    placed = (
        P("dp", None),
        P("dp", ("tensor", "group")),
        P(("tensor", "group"), None),
        P(),
        P(),
        P("dp", None),
        P("tensor", None, ("dp", "group")),
        P("tensor", None, ("dp", "group")),
        P("tensor", ("dp", "group"), None),
        P("dp", None),
    )
    return jax.shard_map(
        functools.partial(on_device, mesh.shape["dp"]),
        mesh=mesh,
        in_specs=placed,
        out_specs=(P("dp", None), P("dp", ("tensor", "group")), P("tensor", ("dp", "group"), None)),
        check_vma=False,
    )
```
